128 devices in a mesh: head: 8 (over y, x_hi), ctx: 16 (over z, x_lo, core).
Axes of the slice: x: 4 (x_hi: 2, x_lo: 2; x = x_hi * 2 + x_lo), y: 4, z: 4, core: 2. Of those that a mesh axis runs over, the one named last changes fastest.
Arguments:
- queries: bfloat16 [2048, 36864], P('ctx', 'head'), may hold values from -12 to 12
- latent_rows: bfloat16 [2048, 576], P('ctx'), may hold values from -4 to 4
- output_grad: bfloat16 [2048, 8192], P('ctx', 'head'), may hold values from -12 to 12
- up_query: bfloat16 [1536, 12288], P(None, 'head'), may hold values from -0.15625 to 0.15625
- up_key: bfloat16 [64, 128, 512], P('head'), may hold values from -0.5 to 0.5
- up_value: bfloat16 [64, 512, 128], P('head'), may hold values from -0.25 to 0.25
- block_order: int32 [32], replicated, may hold values from 0 to 31, each once
Outputs:
- compressed_grad: bfloat16 [2048, 1536], P('ctx', 'head')
- latent_grad: bfloat16 [2048, 576], P('ctx')
The draws below stay inside these ranges and needn't reach their ends.
Inputs may be any that keep to these rules, and one draw needn't show every extreme that they name: `block_order`: every sequence block number appears exactly once.
All inputs are finite; a program needn't handle non-finite values.
Results may differ from the reference program's by a relative error of at most 0.025.
Values may be sent and summed in bfloat16 or wider, within the bound.
No kernel may reach another device: no remote copies, remote signals or barrier semaphores. Data moves between devices by JAX's collectives and lax.ppermute only.
A program may use at most 64 MiB of HBM per device.

```python
import jax
import jax.numpy as jnp
from jax import lax

HEADS = 64
D_LAT = 512
D_ROPE = 64
D_NOPE = 128
D_V = 128
Q_RANK = 1536
BLOCK = 64
TOKENS = 2048
N_CTX = 16


def draw_latent_rows(key, part):
    key = jax.random.fold_in(key, 3)
    row_width = D_LAT + D_ROPE
    values = jnp.clip(jax.random.normal(key, (TOKENS, row_width), jnp.float32), -4.0, 4.0)
    return values.astype(jnp.bfloat16)


def draw_queries(key, part):
    key = jax.random.fold_in(key, 5)
    row_width = D_LAT + D_ROPE
    values = jnp.clip(jax.random.normal(key, (TOKENS, HEADS, row_width), jnp.float32), -4.0, 4.0)
    return values.reshape(TOKENS, HEADS * row_width).astype(jnp.bfloat16)


def block_levels(stream_key, dims, cuts, low, high):
    factor_of = 1.0
    for dim, parts in cuts:
        draws = jax.random.uniform(jax.random.fold_in(jax.random.fold_in(stream_key, 6), dim), (parts,), jnp.float32, low / len(cuts), high / len(cuts))
        factor_of = factor_of * jnp.repeat(jnp.exp(draws), dims[dim] // parts).reshape((-1,) + (1,) * (len(dims) - 1 - dim))
    return factor_of


def bell_draw(rng, extent, scale, reach, shards=(), held_as=jnp.bfloat16):
    loudness = block_levels(rng, extent, shards, -0.22, 0.18) if shards else 1.0
    result = jax.random.normal(rng, extent, jnp.float32) * scale * loudness
    return jnp.minimum(jnp.maximum(result, -reach), reach).astype(held_as)


def setup_inputs(seed: int = 0) -> dict:
    arg_keys = jax.random.split(jax.random.key(seed), 8)
    return {
        "queries": draw_queries(jax.random.fold_in(arg_keys[7], 71), 0),
        "latent_rows": draw_latent_rows(jax.random.fold_in(arg_keys[7], 71), 0),
        "output_grad": bell_draw(arg_keys[2], (TOKENS, HEADS * D_V), 2.0, 12.0, ((0, 16), (1, 8))),
        "up_query": bell_draw(arg_keys[3], (Q_RANK, HEADS * (D_NOPE + D_ROPE)), Q_RANK ** -0.5, 0.15625, ((1, 8),)),
        "up_key": bell_draw(arg_keys[4], (HEADS, D_NOPE, D_LAT), D_NOPE ** -0.5, 0.5, ((0, 8),)),
        "up_value": bell_draw(arg_keys[5], (HEADS, D_LAT, D_V), D_LAT ** -0.5, 0.25, ((0, 8),)),
        "block_order": jax.random.permutation(arg_keys[6], 2 * N_CTX).astype(jnp.int32),
    }


def positions(block_order, rows):
    row_index = jnp.arange(rows, dtype=jnp.int32)
    return block_order[row_index // BLOCK] * BLOCK + row_index % BLOCK


def rope_tables(position):
    half_rope = D_ROPE // 2
    frequency = 10000.0 ** (-(2.0 * jnp.arange(half_rope, dtype=jnp.float32)) / D_ROPE)
    angles = position.astype(jnp.float32)[:, None] * frequency[None, :]
    return jnp.cos(angles), jnp.sin(angles)


def reference(queries, latent_rows, output_grad, up_query, up_key, up_value, block_order):
    position = positions(block_order, TOKENS)
    visible = position[None, :] <= position[:, None]
    cosine_table, sine_table = rope_tables(position)
    softmax_scale = (D_NOPE + D_ROPE) ** -0.5
    row_width = D_LAT + D_ROPE
    half_rope = D_ROPE // 2
    query_heads = queries.reshape(TOKENS, HEADS, row_width).transpose(1, 0, 2)
    grad_heads = output_grad.reshape(TOKENS, HEADS, D_V).transpose(1, 0, 2)

    def one_head(total_keys, inputs):
        query_head, grad_head, key_map, value_map = inputs
        scores = jnp.dot(query_head, latent_rows.T, preferred_element_type=jnp.float32) * softmax_scale
        masked = jnp.where(visible, scores, -jnp.inf)
        row_max = jnp.max(masked, axis=1, keepdims=True)
        exponent = jnp.where(visible, jnp.exp(scores - row_max), 0.0)
        prob = exponent / jnp.sum(exponent, axis=1, keepdims=True)
        value_grad = jnp.dot(grad_head, value_map.T, preferred_element_type=jnp.float32).astype(jnp.bfloat16)
        prob_grad = jnp.dot(value_grad, latent_rows[:, :D_LAT].T, preferred_element_type=jnp.float32)
        row_delta = jnp.sum(prob * prob_grad, axis=1, keepdims=True)
        score_grad = (prob * (prob_grad - row_delta) * softmax_scale).astype(jnp.bfloat16)
        prob_low = prob.astype(jnp.bfloat16)
        query_back = jnp.dot(score_grad, latent_rows, preferred_element_type=jnp.float32).astype(jnp.bfloat16)
        key_grad = jnp.dot(score_grad.T, query_head, preferred_element_type=jnp.float32)
        value_part = jnp.dot(prob_low.T, value_grad, preferred_element_type=jnp.float32)
        key_grad = key_grad + jnp.pad(value_part, ((0, 0), (0, D_ROPE)))
        nope_grad = jnp.dot(query_back[:, :D_LAT], key_map.T, preferred_element_type=jnp.float32)
        rope_grad = query_back[:, D_LAT:].astype(jnp.float32)
        low_half = rope_grad[:, :half_rope]
        high_half = rope_grad[:, half_rope:]
        rope_back = jnp.concatenate([low_half * cosine_table + high_half * sine_table,
                                     high_half * cosine_table - low_half * sine_table], axis=1)
        full_grad = jnp.concatenate([nope_grad, rope_back], axis=1).astype(jnp.bfloat16)
        return total_keys + key_grad, full_grad

    start_keys = jnp.zeros((TOKENS, row_width), jnp.float32)
    total_keys, head_grads = lax.scan(one_head, start_keys, (query_heads, grad_heads, up_key, up_value))
    joined = head_grads.transpose(1, 0, 2).reshape(TOKENS, HEADS * (D_NOPE + D_ROPE))
    compressed_grad = jnp.dot(joined, up_query.T, preferred_element_type=jnp.float32).astype(jnp.bfloat16)
    return compressed_grad, total_keys.astype(jnp.bfloat16)
```

```python
import functools

import jax
import jax.numpy as jnp
from jax import lax
from jax.experimental import pallas as pl
from jax.experimental.pallas import tpu as pltpu
from jax.sharding import Mesh
from jax.sharding import PartitionSpec as P

D_LAT = 512
D_ROPE = 64
D_NOPE = 128
D_V = 128
BLOCK = 64
ROW = D_LAT + D_ROPE
HALF = D_ROPE // 2
N_Y, N_XH, N_Z, N_XL = 4, 2, 4, 2
TOK = 128
HEADS_L = 8
SHARDS = N_Z * N_XL
KEYS = SHARDS * TOK
ROWS = 2 * HEADS_L * TOK
HROWS = HEADS_L * TOK
F_ROWS = HEADS_L * (D_NOPE + D_ROPE)
C_COLS = 192
SCALE = (D_NOPE + D_ROPE) ** -0.5
LOG2E = 1.4426950408889634
MASKED = -1e30
AXES = ("y", "xh", "z", "xl", "core")
VMEM_LIMIT = 56 * 1024 * 1024
TN = 256

SHIFTS = ((0, 1, 0), (0, 3, 0), (0, 0, 1), (0, 2, 0), (1, 1, 1), (0, 3, 1), (1, 2, 1))

NT = (((1,), (1,)), ((), ()))
NN = (((1,), (0,)), ((), ()))
bf16 = jnp.bfloat16
f32 = jnp.float32


def dot(a, b, dims=NN):
    return lax.dot_general(a, b, dims, preferred_element_type=f32)


def shift(x, dy=0, dxh=0, dz=0, dxl=0, dcore=0):
    pairs = []
    dims = (N_Y, N_XH, N_Z, N_XL, 2)
    deltas = (dy, dxh, dz, dxl, dcore)
    for source in range(N_Y * N_XH * N_Z * N_XL * 2):
        rest, coords = source, []
        for n in reversed(dims):
            coords.append(rest % n)
            rest //= n
        coords.reverse()
        target = 0
        for n, c, d in zip(dims, coords, deltas):
            target = target * n + (c + d) % n
        pairs.append((source, target))
    return lax.ppermute(x, AXES, pairs)


def params(**kw):
    return pltpu.CompilerParams(vmem_limit_bytes=VMEM_LIMIT, **kw)


def vmem():
    return pl.BlockSpec(memory_space=pltpu.VMEM)


def smem():
    return pl.BlockSpec(memory_space=pltpu.SMEM)


def prologue_kernel(q0, q1, do0, do1, uv, qt, gt):
    for s, (q, do) in enumerate(((q0, do0), (q1, do1))):
        for j in range(HEADS_L * ROW // 128):
            t = q[:, j * 128 : (j + 1) * 128].T
            for k in range(2):
                r = j * 128 + k * 64
                h, d = r // ROW, r % ROW
                col = (s * HEADS_L + h) * TOK
                qt[d : d + 64, col : col + TOK] = t[k * 64 : (k + 1) * 64, :]
        for h in range(HEADS_L):
            col = (s * HEADS_L + h) * TOK
            g = dot(uv[h], do[:, h * D_V : (h + 1) * D_V], NT)
            gt[:, col : col + TOK] = g.astype(bf16)


def prologue(q0, q1, do0, do1, uv):
    return pl.pallas_call(
        prologue_kernel,
        out_shape=(
            jax.ShapeDtypeStruct((ROW, ROWS), bf16),
            jax.ShapeDtypeStruct((D_LAT, ROWS), bf16),
        ),
        in_specs=[vmem()] * 5,
        out_specs=(vmem(), vmem()),
        compiler_params=params(),
        cost_estimate=pl.CostEstimate(
            flops=2 * ROWS * D_V * D_LAT, bytes_accessed=9 * 1024 * 1024, transcendentals=0
        ),
        name="prologue",
    )(q0, q1, do0, do1, uv)


def scores_kernel(kblk, qblk, *refs):
    kts = refs[:SHARDS]
    qt, gt, e_out, dp_out, m_out, merged, k_nat, bias = refs[SHARDS:]

    @pl.when(pl.program_id(0) == 0)
    def _():
        for s in range(SHARDS):
            for j in range(4):
                k_nat[s * TOK : (s + 1) * TOK, j * 128 : (j + 1) * 128] = kts[s][
                    j * 128 : (j + 1) * 128, :
                ].T
            k_nat[s * TOK : (s + 1) * TOK, D_LAT:ROW] = kts[s][D_LAT:ROW, :].T
        lane = lax.broadcasted_iota(jnp.int32, (BLOCK, TOK), 1)
        sub = lax.broadcasted_iota(jnp.int32, (BLOCK, TOK), 0)
        for t in range(2):
            q_pos = jnp.where(
                lane < BLOCK, qblk[2 * t] * BLOCK + lane, qblk[2 * t + 1] * BLOCK + lane - BLOCK
            )
            for b in range(2 * SHARDS):
                k_pos = kblk[b] * BLOCK + sub
                bias[t, b * BLOCK : (b + 1) * BLOCK, :] = jnp.where(k_pos <= q_pos, 0.0, MASKED)

    token_set = pl.program_id(0) // (HROWS // TN)
    k_scale = SCALE * LOG2E
    ms, ls, ws = [], [], []
    for s in range(SHARDS):
        rows = slice(s * TOK, (s + 1) * TOK)
        sc = dot(k_nat[rows, :], qt[...])
        dp = dot(k_nat[rows, :D_LAT], gt[...])
        b = bias[token_set, rows, :]
        for j in range(TN // TOK):
            cols = slice(j * TOK, (j + 1) * TOK)
            x = sc[:, cols] * k_scale + b
            m = jnp.max(x, axis=0, keepdims=True)
            e = jnp.exp2(x - m)
            d = dp[:, cols]
            l = jnp.sum(e, axis=0, keepdims=True)
            w = jnp.sum(e * d, axis=0, keepdims=True)
            e_out[rows, cols] = e.astype(bf16)
            dp_out[rows, cols] = d.astype(bf16)
            m_out[s : s + 1, cols] = m
            ms.append(m)
            ls.append(l)
            ws.append(w)
    n = TN // TOK
    for j in range(n):
        cols = slice(j * TOK, (j + 1) * TOK)
        mj, lj, wj = ms[j::n], ls[j::n], ws[j::n]
        top = functools.reduce(jnp.maximum, mj)
        f = [jnp.exp2(m - top) for m in mj]
        merged[0:1, cols] = top
        merged[1:2, cols] = sum(a * b for a, b in zip(f, lj))
        merged[2:3, cols] = sum(a * b for a, b in zip(f, wj))


def scores(kblk, qblk, kts, qt, gt):
    return pl.pallas_call(
        scores_kernel,
        grid=(ROWS // TN,),
        out_shape=(
            jax.ShapeDtypeStruct((KEYS, ROWS), bf16),
            jax.ShapeDtypeStruct((KEYS, ROWS), bf16),
            jax.ShapeDtypeStruct((SHARDS, ROWS), f32),
            jax.ShapeDtypeStruct((8, ROWS), f32),
        ),
        in_specs=[smem(), smem()]
        + [pl.BlockSpec((ROW, TOK), lambda i: (0, 0))] * SHARDS
        + [pl.BlockSpec((ROW, TN), lambda i: (0, i)), pl.BlockSpec((D_LAT, TN), lambda i: (0, i))],
        out_specs=(
            pl.BlockSpec((KEYS, TN), lambda i: (0, i)),
            pl.BlockSpec((KEYS, TN), lambda i: (0, i)),
            pl.BlockSpec((SHARDS, TN), lambda i: (0, i)),
            pl.BlockSpec((8, TN), lambda i: (0, i)),
        ),
        scratch_shapes=[pltpu.VMEM((KEYS, ROW), bf16), pltpu.VMEM((2, KEYS, TOK), f32)],
        compiler_params=params(),
        cost_estimate=pl.CostEstimate(
            flops=2 * ROWS * KEYS * (ROW + D_LAT),
            bytes_accessed=14 * 1024 * 1024,
            transcendentals=ROWS * KEYS,
        ),
        name="scores",
    )(kblk, qblk, *kts, qt, gt)


def grads_kernel(e, dp, m, mine, theirs, qt, gt, *refs):
    outs = refs[:2]
    ds_out, r_s, rc_s, delta_s, p_s = refs[2:]

    @pl.when(pl.program_id(0) == 0)
    def _():
        for j in range(2):
            a = slice(j * HROWS, (j + 1) * HROWS)
            b = slice((1 - j) * HROWS, (2 - j) * HROWS)
            m0, m1 = mine[0:1, a], theirs[0:1, b]
            top = jnp.maximum(m0, m1)
            f0, f1 = jnp.exp2(m0 - top), jnp.exp2(m1 - top)
            inv = 1.0 / (f0 * mine[1:2, a] + f1 * theirs[1:2, b])
            delta_s[0:1, a] = (f0 * mine[2:3, a] + f1 * theirs[2:3, b]) * inv
            r = jnp.exp2(m[:, a] - top) * inv
            r_s[:, a] = r
            rc_s[:, a] = r * SCALE

    step = pl.program_id(0)
    for k in range(2):
        rows = slice(k * TOK, (k + 1) * TOK)
        for j in range(ROWS // TN):
            cols = slice(j * TN, (j + 1) * TN)
            ef = e[rows, cols].astype(f32)
            r = r_s[pl.ds(step * 2 + k, 1), cols]
            rc = rc_s[pl.ds(step * 2 + k, 1), cols]
            p_s[rows, cols] = (ef * r).astype(bf16)
            ds_out[rows, cols] = (
                ef * rc * (dp[rows, cols].astype(f32) - delta_s[0:1, cols])
            ).astype(bf16)
    dk = dot(qt[...], ds_out[...], NT)
    dv = dot(gt[...], p_s[...], NT)
    for k in range(2):
        cols = slice(k * TOK, (k + 1) * TOK)
        outs[k][0, :D_LAT, :] = (dk[:D_LAT, cols] + dv[:, cols]).astype(bf16)
        outs[k][0, D_LAT:, :] = dk[D_LAT:, cols].astype(bf16)


def grads(e, dp, m, mine, theirs, qt, gt):
    full = lambda shape: pl.BlockSpec(shape, lambda i: (0,) * len(shape))
    steps = SHARDS // 2
    return pl.pallas_call(
        grads_kernel,
        grid=(steps,),
        out_shape=(
            jax.ShapeDtypeStruct((steps, ROW, TOK), bf16),
            jax.ShapeDtypeStruct((steps, ROW, TOK), bf16),
            jax.ShapeDtypeStruct((KEYS, ROWS), bf16),
        ),
        in_specs=[
            pl.BlockSpec((2 * TOK, ROWS), lambda i: (i, 0)),
            pl.BlockSpec((2 * TOK, ROWS), lambda i: (i, 0)),
            full((SHARDS, ROWS)),
            full((8, ROWS)),
            full((8, ROWS)),
            full((ROW, ROWS)),
            full((D_LAT, ROWS)),
        ],
        out_specs=(
            pl.BlockSpec((1, ROW, TOK), lambda i: (i, 0, 0)),
            pl.BlockSpec((1, ROW, TOK), lambda i: (i, 0, 0)),
            pl.BlockSpec((2 * TOK, ROWS), lambda i: (i, 0)),
        ),
        scratch_shapes=[
            pltpu.VMEM((SHARDS, ROWS), f32),
            pltpu.VMEM((SHARDS, ROWS), f32),
            pltpu.VMEM((8, ROWS), f32),
            pltpu.VMEM((2 * TOK, ROWS), bf16),
        ],
        compiler_params=params(),
        cost_estimate=pl.CostEstimate(
            flops=2 * ROWS * KEYS * (ROW + D_LAT),
            bytes_accessed=18 * 1024 * 1024,
            transcendentals=0,
        ),
        name="grads",
    )(e, dp, m, mine, theirs, qt, gt)


def query_kernel(*refs):
    kts = refs[:SHARDS]
    ds, out, kt = refs[SHARDS:]

    @pl.when(pl.program_id(0) == 0)
    def _():
        for s in range(SHARDS):
            kt[:, s * TOK : (s + 1) * TOK] = kts[s][...]

    out[...] = dot(kt[...], ds[...]).astype(bf16)


def query_grad(kts, ds, token_set):
    steps = HROWS // TN
    return pl.pallas_call(
        query_kernel,
        grid=(steps,),
        out_shape=jax.ShapeDtypeStruct((ROW, HROWS), bf16),
        in_specs=[pl.BlockSpec((ROW, TOK), lambda i: (0, 0))] * SHARDS
        + [pl.BlockSpec((KEYS, TN), lambda i: (0, i + token_set * steps))],
        out_specs=pl.BlockSpec((ROW, TN), lambda i: (0, i)),
        scratch_shapes=[pltpu.VMEM((ROW, KEYS), bf16)],
        compiler_params=params(),
        cost_estimate=pl.CostEstimate(
            flops=2 * HROWS * KEYS * ROW, bytes_accessed=4 * 1024 * 1024, transcendentals=0
        ),
        name="query_grad",
    )(*kts, ds)


def project_kernel(place, own, got, cos, sin, uk, uq_hbm, send, keep, uq, ft, cg, sem):
    copy = pltpu.make_async_copy(uq_hbm, uq, sem)
    copy.start()
    for h in range(HEADS_L):
        cols = slice(h * TOK, (h + 1) * TOK)
        d = (own[:, cols].astype(f32) + got[:, cols].astype(f32)).astype(bf16)
        base = h * (D_NOPE + D_ROPE)
        ft[base : base + D_NOPE, :] = dot(uk[h], d[:D_LAT]).astype(bf16)
        a = d[D_LAT : D_LAT + HALF].astype(f32)
        b = d[D_LAT + HALF :].astype(f32)
        base += D_NOPE
        ft[base : base + HALF, :] = (a * cos[...] + b * sin[...]).astype(bf16)
        ft[base + HALF : base + D_ROPE, :] = (b * cos[...] - a * sin[...]).astype(bf16)
    copy.wait()
    cg[...] = dot(uq[...], ft[...]).astype(bf16)
    y, xh = place[0], place[1]
    for d in range(N_Y):
        yd = lax.rem(y + d, N_Y)
        send[d] = cg[pl.ds(pl.multiple_of((yd * 2 + 1 - xh) * C_COLS, 64), C_COLS), :]
        keep[d] = cg[pl.ds(pl.multiple_of((yd * 2 + xh) * C_COLS, 64), C_COLS), :]


def project(place, own, got, cos, sin, uk, uq):
    q_rank = uq.shape[0]
    return pl.pallas_call(
        project_kernel,
        out_shape=(
            jax.ShapeDtypeStruct((N_Y, C_COLS, TOK), bf16),
            jax.ShapeDtypeStruct((N_Y, C_COLS, TOK), bf16),
        ),
        in_specs=[smem()] + [vmem()] * 5 + [pl.BlockSpec(memory_space=pl.ANY)],
        out_specs=(vmem(), vmem()),
        scratch_shapes=[
            pltpu.VMEM((q_rank, F_ROWS), bf16),
            pltpu.VMEM((F_ROWS, TOK), bf16),
            pltpu.VMEM((q_rank, TOK), bf16),
            pltpu.SemaphoreType.DMA,
        ],
        compiler_params=params(),
        cost_estimate=pl.CostEstimate(
            flops=2 * TOK * F_ROWS * q_rank + 2 * HROWS * D_LAT * D_NOPE,
            bytes_accessed=9 * 1024 * 1024,
            transcendentals=0,
        ),
        name="project",
    )(place, own, got, cos, sin, uk, uq)


def per_device(queries, latent_rows, output_grad, up_query, up_key, up_value, block_order):
    y, xh = lax.axis_index("y"), lax.axis_index("xh")
    z, xl, core = lax.axis_index("z"), lax.axis_index("xl"), lax.axis_index("core")

    def place(z, xl, c):
        return (z * N_XL + xl) * 2 + c

    own_kt = latent_rows.T
    q_other = shift(queries, dcore=1)
    do_other = shift(output_grad, dcore=1)
    kts = [own_kt] + [shift(own_kt, dxh=a, dz=b, dxl=c) for a, b, c in SHIFTS]
    owners = [place(z, xl, core)] + [
        place((z - b) % N_Z, (xl - c) % N_XL, core) for _, b, c in SHIFTS
    ]
    order2 = block_order.reshape(-1, 2)
    kblk = order2[jnp.stack(owners)].reshape(-1)
    qblk = order2[jnp.stack([place(z, xl, core), place(z, xl, 1 - core)])].reshape(-1)
    token = jnp.arange(TOK, dtype=jnp.int32)
    pos = jnp.where(token < BLOCK, qblk[0] * BLOCK + token, qblk[1] * BLOCK + token - BLOCK)
    frequency = 10000.0 ** (-(2.0 * jnp.arange(HALF, dtype=f32)) / D_ROPE)
    angles = pos.astype(f32)[None, :] * frequency[:, None]
    cos, sin = jnp.cos(angles), jnp.sin(angles)

    qt, gt = prologue(queries, q_other, output_grad, do_other, up_value)
    e, dp, m, mine = scores(kblk, qblk, kts, qt, gt)
    theirs = shift(mine, dcore=1)
    dk_even, dk_odd, ds = grads(e, dp, m, mine, theirs, qt, gt)

    total = dk_even[0].astype(f32)
    for i, (a, b, c) in enumerate(SHIFTS, 1):
        part = (dk_even, dk_odd)[i % 2][i // 2]
        total = total + shift(part, dxh=-a, dz=-b, dxl=-c).astype(f32)
    total = total.astype(bf16)

    dq_other = shift(query_grad(kts, ds, 1), dcore=1)
    dq_own = query_grad(kts, ds, 0)
    send, keep = project(jnp.stack([y, xh]), dq_own, dq_other, cos, sin, up_key, up_query)
    cg = (keep.astype(f32) + shift(send, dxh=1).astype(f32)).astype(bf16)
    part = [cg[0]] + [shift(cg[d], dy=d) for d in range(1, N_Y)]
    cg = sum(p.astype(f32) for p in part).astype(bf16)

    total = (total.astype(f32) + shift(total, dxh=1).astype(f32)).astype(bf16)
    s1, s2, s3 = (shift(total, dy=d).astype(f32) for d in range(1, N_Y))
    total = ((total.astype(f32) + s2) + (s1 + s3)).astype(bf16)
    return cg.T, total.T


def solution(mesh):
    fine = Mesh(mesh.devices.reshape(N_Y, N_XH, N_Z, N_XL, 2), AXES)
    head, ctx = ("y", "xh"), ("z", "xl", "core")
    in_specs = (
        P(ctx, head),
        P(ctx, None),
        P(ctx, head),
        P(None, head),
        P(head, None, None),
        P(head, None, None),
        P(),
    )
    out_specs = (P(ctx, head), P(ctx, None))
    return jax.shard_map(
        per_device, mesh=fine, in_specs=in_specs, out_specs=out_specs, check_vma=False
    )
```

```python
import functools

import jax
import jax.numpy as jnp
from jax import lax
from jax.experimental import pallas as pl
from jax.experimental.pallas import tpu as pltpu
from jax.sharding import Mesh
from jax.sharding import PartitionSpec as P

D_LAT = 512
D_ROPE = 64
D_NOPE = 128
D_V = 128
BLOCK = 64
ROW = D_LAT + D_ROPE
HALF = D_ROPE // 2
N_Y, N_XH, N_Z, N_XL = 4, 2, 4, 2
N_X = N_XH * N_XL
TOK = 128
HEADS_L = 8
SHARDS = N_Z * N_XL
KEYS = SHARDS * TOK
HROWS = HEADS_L * TOK
ROWS = 2 * HROWS
F_ROWS = HEADS_L * (D_NOPE + D_ROPE)
C_COLS = 192
SCALE = (D_NOPE + D_ROPE) ** -0.5
K_SCALE = SCALE * 1.4426950408889634
MASKED = -1e30
AXES = ("y", "xh", "z", "xl", "core")
TN = 256

SLOTS = ((0, 0), (0, 1), (1, 0), (3, 0), (2, 0), (1, 1), (3, 1), (2, 1))
EARLY = 4

NT = (((1,), (1,)), ((), ()))
NN = (((1,), (0,)), ((), ()))
bf16 = jnp.bfloat16
f32 = jnp.float32


def dot(a, b, dims=NN):
    return lax.dot_general(a, b, dims, preferred_element_type=f32)


def shift(x, dy=0, dx=0, dz=0, dxl=0, dcore=0):
    pairs = []
    for y in range(N_Y):
        for xh in range(N_XH):
            for z in range(N_Z):
                for xl in range(N_XL):
                    for c in range(2):
                        a = (xh * N_XL + xl + dx) % N_X
                        to = ((y + dy) % N_Y) * N_XH + a // N_XL
                        to = to * N_Z + (z + dz) % N_Z
                        to = to * N_XL + (a + dxl) % N_XL
                        to = to * 2 + (c + dcore) % 2
                        pairs.append((len(pairs), to))
    return lax.ppermute(x, AXES, pairs)


def params(mib):
    return pltpu.CompilerParams(vmem_limit_bytes=mib * 1024 * 1024)


def cost(flops, exps=0):
    return pl.CostEstimate(flops=flops, bytes_accessed=1024 * 1024, transcendentals=exps)


def vmem():
    return pl.BlockSpec(memory_space=pltpu.VMEM)


def smem():
    return pl.BlockSpec(memory_space=pltpu.SMEM)


def hbm():
    return pl.BlockSpec(memory_space=pltpu.HBM)


def like(*shape, dtype=bf16):
    return jax.ShapeDtypeStruct(shape, dtype)


def kept(*shape, dtype=bf16):
    return pltpu.VMEM(shape, dtype)


def held(*arrays):
    return [pltpu.with_memory_space_constraint(x, pltpu.VMEM) for x in arrays]


def left(x):
    return pltpu.with_memory_space_constraint(x, pltpu.HBM)


def prologue_kernel(q0, q1, do0, do1, uv_hbm, qt, gt, q_own, do_own, uv, sems):
    copies = [
        pltpu.make_async_copy(src, dst, sems.at[i])
        for i, (src, dst) in enumerate(((uv_hbm, uv), (do0, do_own), (q0, q_own)))
    ]
    for c in copies:
        c.start()

    def transpose(s, q):
        for j in range(HEADS_L * ROW // 128):
            t = q[:, j * 128 : (j + 1) * 128].T
            for k in range(2):
                r = j * 128 + k * 64
                h, d = r // ROW, r % ROW
                col = (s * HEADS_L + h) * TOK
                qt[d : d + 64, col : col + TOK] = t[k * 64 : (k + 1) * 64, :]

    def value_grad(s, do):
        for h in range(HEADS_L):
            col = (s * HEADS_L + h) * TOK
            g = dot(uv[h], do[:, h * D_V : (h + 1) * D_V], NT)
            gt[:, col : col + TOK] = g.astype(bf16)

    transpose(1, q1)
    copies[0].wait()
    value_grad(1, do1)
    copies[1].wait()
    value_grad(0, do_own)
    copies[2].wait()
    transpose(0, q_own)


def prologue(q0, q1, do0, do1, uv):
    return pl.pallas_call(
        prologue_kernel,
        out_shape=(kept(ROW, ROWS), kept(D_LAT, ROWS)),
        in_specs=[hbm(), vmem(), hbm(), vmem(), hbm()],
        out_specs=(vmem(), vmem()),
        scratch_shapes=[
            pltpu.VMEM(q0.shape, bf16),
            pltpu.VMEM(do0.shape, bf16),
            pltpu.VMEM(uv.shape, bf16),
            pltpu.SemaphoreType.DMA((3,)),
        ],
        compiler_params=params(10),
        cost_estimate=cost(2 * ROWS * D_V * D_LAT),
        name="prologue",
    )(left(q0), q1, left(do0), do1, left(uv))


def scores_kernel(slots, order, place, qt, gt, *refs):
    n = len(slots)
    kts, refs = refs[:n], refs[n:]
    before = None
    if slots[0]:
        before, refs = refs[0], refs[1:]
    e_out, dp_out, kt_out, m_out, merged, k_nat, bias = refs
    z, xl, core = place[0], place[1], place[2]

    def owner(dz, dxl, c):
        return (lax.rem(z + N_Z - dz, N_Z) * N_XL + lax.rem(xl + dxl, N_XL)) * 2 + c

    lane = lax.broadcasted_iota(jnp.int32, (BLOCK, TOK), 1)
    sub = lax.broadcasted_iota(jnp.int32, (BLOCK, TOK), 0)
    for i, slot in enumerate(slots):
        k_nat[i * TOK : (i + 1) * TOK, :] = kts[i][...].T
        kt_out[:, i * TOK : (i + 1) * TOK] = kts[i][...]
        o = owner(*SLOTS[slot], core)
        for t in range(2):
            q = owner(0, 0, core if t == 0 else 1 - core)
            q_pos = jnp.where(
                lane < BLOCK,
                order[2 * q] * BLOCK + lane,
                order[2 * q + 1] * BLOCK + lane - BLOCK,
            )
            for b in range(2):
                k_pos = order[2 * o + b] * BLOCK + sub
                at = i * TOK + b * BLOCK
                bias[t, at : at + BLOCK, :] = jnp.where(k_pos <= q_pos, 0.0, MASKED)

    @pl.loop(0, ROWS // TN)
    def _(step):
        base = pl.multiple_of(step * TN, TN)
        token_set = step // (HROWS // TN)
        q, g = qt[:, pl.ds(base, TN)], gt[:, pl.ds(base, TN)]
        halves = TN // TOK
        ms, ls, ws = [], [], []
        for i in range(n):
            rows = slice(i * TOK, (i + 1) * TOK)
            sc = dot(k_nat[rows, :], q)
            dp = dot(k_nat[rows, :D_LAT], g)
            b = bias[token_set, rows, :]
            for j in range(halves):
                cols = pl.ds(base + j * TOK, TOK)
                x = sc[:, j * TOK : (j + 1) * TOK] * K_SCALE + b
                m = jnp.max(x, axis=0, keepdims=True)
                e = jnp.exp2(x - m)
                d = dp[:, j * TOK : (j + 1) * TOK]
                ms.append(m)
                ls.append(jnp.sum(e, axis=0, keepdims=True))
                ws.append(jnp.sum(e * d, axis=0, keepdims=True))
                e_out[rows, cols] = e.astype(bf16)
                dp_out[rows, cols] = d.astype(bf16)
                m_out[i : i + 1, cols] = m
        for j in range(halves):
            cols = pl.ds(base + j * TOK, TOK)
            mj, lj, wj = ms[j::halves], ls[j::halves], ws[j::halves]
            if before is not None:
                mj, lj, wj = (
                    a + [before[k : k + 1, cols]] for k, a in enumerate((mj, lj, wj))
                )
            top = functools.reduce(jnp.maximum, mj)
            f = [jnp.exp2(m - top) for m in mj]
            merged[0:1, cols] = top
            merged[1:2, cols] = sum(a * b for a, b in zip(f, lj))
            merged[2:3, cols] = sum(a * b for a, b in zip(f, wj))


def scores(slots, order, place, qt, gt, kts, before=()):
    n = len(slots)
    return pl.pallas_call(
        functools.partial(scores_kernel, slots),
        out_shape=(
            kept(n * TOK, ROWS),
            kept(n * TOK, ROWS),
            kept(ROW, n * TOK),
            like(8, ROWS, dtype=f32),
            like(8, ROWS, dtype=f32),
        ),
        in_specs=[smem(), smem()] + [vmem()] * (2 + n + len(before)),
        out_specs=(vmem(),) * 5,
        scratch_shapes=[pltpu.VMEM((n * TOK, ROW), bf16), pltpu.VMEM((2, n * TOK, TOK), f32)],
        compiler_params=params(8),
        cost_estimate=cost(2 * ROWS * n * TOK * (ROW + D_LAT), ROWS * n * TOK),
        name="scores",
    )(order, place, *held(qt, gt), *kts, *before)


def grads_kernel(counts, *refs):
    n = len(counts)
    es, dps, ms, refs = refs[:n], refs[n : 2 * n], refs[2 * n : 3 * n], refs[3 * n :]
    mine, theirs, qt, gt = refs[:4]
    outs, refs = refs[4 : 4 + N_Z], refs[4 + N_Z :]
    dss, (r_s, rc_s, delta_s, p_s, dk_s, sems) = refs[:n], refs[n:]
    copies = []
    for j in range(2):
        a = slice(j * HROWS, (j + 1) * HROWS)
        b = slice((1 - j) * HROWS, (2 - j) * HROWS)
        m0, m1 = mine[0:1, a], theirs[0:1, b]
        top = jnp.maximum(m0, m1)
        f0, f1 = jnp.exp2(m0 - top), jnp.exp2(m1 - top)
        inv = 1.0 / (f0 * mine[1:2, a] + f1 * theirs[1:2, b])
        delta_s[0:1, a] = (f0 * mine[2:3, a] + f1 * theirs[2:3, b]) * inv
        at = 0
        for m, c in zip(ms, counts):
            r = jnp.exp2(m[:c, a] - top) * inv
            r_s[at : at + c, a] = r
            rc_s[at : at + c, a] = r * SCALE
            at += c
    at = 0
    for e, dp, ds, c in zip(es, dps, dss, counts):
        for k in range(c):
            s = at + k
            rows = slice(k * TOK, (k + 1) * TOK)
            p_rows = slice((s % 4) * TOK, (s % 4 + 1) * TOK)
            for j in range(ROWS // TN):
                cols = slice(j * TN, (j + 1) * TN)
                ef = e[rows, cols].astype(f32)
                p_s[p_rows, cols] = (ef * r_s[s : s + 1, cols]).astype(bf16)
                d = dp[rows, cols].astype(f32) - delta_s[0:1, cols]
                ds[rows, cols] = (ef * rc_s[s : s + 1, cols] * d).astype(bf16)
            if k % 2:
                pair = slice((k - 1) * TOK, (k + 1) * TOK)
                p_pair = slice((s % 4 - 1) * TOK, (s % 4 + 1) * TOK)
                dk = dot(qt[...], ds[pair, :], NT)
                dv = dot(gt[...], p_s[p_pair, :], NT)
                for i in range(2):
                    h = slice(i * TOK, (i + 1) * TOK)
                    o = s - 1 + i
                    dz, dxl = SLOTS[o]
                    dk_s[o, :D_LAT, :] = (dk[:D_LAT, h] + dv[:, h]).astype(bf16)
                    dk_s[o, D_LAT:, :] = dk[D_LAT:, h].astype(bf16)
                    copies.append(pltpu.make_async_copy(dk_s.at[o], outs[dz].at[dxl], sems.at[o]))
                    copies[-1].start()
        at += c
    for copy in copies:
        copy.wait()


def grads(parts, mine, theirs, qt, gt):
    es, dps, ms = zip(*parts)
    counts = tuple(e.shape[0] // TOK for e in es)
    res = pl.pallas_call(
        functools.partial(grads_kernel, counts),
        out_shape=(pltpu.HBM((N_XL, ROW, TOK), bf16),) * N_Z + tuple(kept(*e.shape) for e in es),
        in_specs=[vmem()] * (3 * len(parts) + 4),
        out_specs=(hbm(),) * N_Z + (vmem(),) * len(parts),
        scratch_shapes=[
            pltpu.VMEM((SHARDS, ROWS), f32),
            pltpu.VMEM((SHARDS, ROWS), f32),
            pltpu.VMEM((8, ROWS), f32),
            pltpu.VMEM((4 * TOK, ROWS), bf16),
            pltpu.VMEM((SHARDS, ROW, TOK), bf16),
            pltpu.SemaphoreType.DMA((SHARDS,)),
        ],
        compiler_params=params(8),
        cost_estimate=cost(2 * ROWS * KEYS * (ROW + D_LAT)),
        name="grads",
    )(*held(*es, *dps), *ms, mine, theirs, *held(qt, gt))
    return res[:N_Z], res[N_Z:]


def project_kernel(place, uk, uq, cos, sin, *refs):
    n = (len(refs) - 6) // 2
    dss, kts = refs[:n], refs[n : 2 * n]
    give_send, give_keep, send, keep, ft, cg = refs[2 * n :]
    for t in (1, 0):
        half = slice(t * HROWS, (t + 1) * HROWS)
        dq = sum(dot(kt[...], ds[:, half]) for kt, ds in zip(kts, dss)).astype(bf16)
        out = slice(t * TOK, (t + 1) * TOK)
        for h in range(HEADS_L):
            d = dq[:, h * TOK : (h + 1) * TOK]
            base = h * (D_NOPE + D_ROPE)
            ft[base : base + D_NOPE, out] = dot(uk[h], d[:D_LAT]).astype(bf16)
            a = d[D_LAT : D_LAT + HALF].astype(f32)
            b = d[D_LAT + HALF :].astype(f32)
            base += D_NOPE
            c, s = cos[:, out], sin[:, out]
            ft[base : base + HALF, out] = (a * c + b * s).astype(bf16)
            ft[base + HALF : base + D_ROPE, out] = (b * c - a * s).astype(bf16)
    cg[...] = dot(uq[...], ft[...]).astype(bf16)
    y, xh = place[3], place[4]
    for d in range(N_Y):
        yd = lax.rem(y + d, N_Y)
        away = pl.ds(pl.multiple_of((yd * 2 + 1 - xh) * C_COLS, 64), C_COLS)
        here = pl.ds(pl.multiple_of((yd * 2 + xh) * C_COLS, 64), C_COLS)
        send[d], keep[d] = cg[away, :TOK], cg[here, :TOK]
        give_send[d], give_keep[d] = cg[away, TOK:], cg[here, TOK:]


def project(place, dss, kts, cos, sin, uk, uq):
    q_rank = uq.shape[0]
    return pl.pallas_call(
        project_kernel,
        out_shape=(like(N_Y, C_COLS, TOK),) * 4,
        in_specs=[smem()] + [vmem()] * (4 + 2 * len(dss)),
        out_specs=(vmem(),) * 4,
        scratch_shapes=[pltpu.VMEM((F_ROWS, 2 * TOK), bf16), pltpu.VMEM((q_rank, 2 * TOK), bf16)],
        compiler_params=params(12),
        cost_estimate=cost(4 * HROWS * KEYS * ROW),
        name="project",
    )(place, uk, uq, cos, sin, *held(*dss, *kts))


def combine_kernel(a, a2, b1, b3, c0, c1, c2, c3, *outs):
    total = (a[...].astype(f32) + a2[...].astype(f32)) + (b1[...].astype(f32) + b3[...].astype(f32))
    total = total.astype(bf16)
    for d in range(N_Y):
        outs[d][:ROW, :] = total
        cg = (c0[d].astype(f32) + c1[d].astype(f32)) + (c2[d].astype(f32) + c3[d].astype(f32))
        outs[d][ROW:, :] = cg.astype(bf16)


def combine(*args):
    return pl.pallas_call(
        combine_kernel,
        out_shape=(like(ROW + C_COLS, TOK),) * N_Y,
        in_specs=[vmem()] * 8,
        out_specs=(vmem(),) * N_Y,
        compiler_params=params(8),
        cost_estimate=cost(1024 * 1024),
        name="combine",
    )(*args)


def add(*parts):
    return sum(p.astype(f32) for p in parts).astype(bf16)


def per_device(queries, latent_rows, output_grad, up_query, up_key, up_value, block_order):
    coords = [lax.axis_index(a) for a in ("z", "xl", "core", "y", "xh")]
    place = jnp.stack(coords).astype(jnp.int32)
    z, xl, core = coords[:3]

    own = latent_rows.T
    q_other = shift(queries, dcore=1)
    do_other = shift(output_grad, dcore=1)
    across = shift(own, dxl=1)
    kts = [own, across]
    kts += [shift(own, dz=dz) for dz, _ in SLOTS[2:5]]
    kts += [shift(across, dz=dz) for dz, _ in SLOTS[5:]]

    first = (z * N_XL + xl) * 4
    near = lax.dynamic_slice(block_order, (first,), (4,))
    near = jnp.where(core == 0, near, jnp.roll(near, 2))
    token = jnp.arange(BLOCK, dtype=jnp.int32)
    pos = (near[:, None] * BLOCK + token).reshape(-1)
    frequency = 10000.0 ** (-(2.0 * jnp.arange(HALF, dtype=f32)) / D_ROPE)
    angles = pos.astype(f32)[None, :] * frequency[:, None]
    cos, sin = jnp.cos(angles), jnp.sin(angles)

    qt, gt = prologue(queries, q_other, output_grad, do_other, up_value)
    near, far = tuple(range(EARLY)), tuple(range(EARLY, SHARDS))
    *part0, kt0, m0, merged = scores(near, block_order, place, qt, gt, kts[:EARLY])
    *part1, kt1, m1, mine = scores(far, block_order, place, qt, gt, kts[EARLY:], (merged,))
    theirs = shift(mine, dcore=1)
    dk, dss = grads(((*part0, m0), (*part1, m1)), mine, theirs, qt, gt)

    from_z = [shift(dk[dz], dz=-dz) for dz in range(1, N_Z)]
    a, b = (add(*(p[i] for p in (dk[0], *from_z))) for i in range(N_XL))

    give_send, give_keep, send, keep = project(place, dss, (kt0, kt1), cos, sin, up_key, up_query)

    b1, b3, a2 = shift(b, dx=1), shift(b, dx=3), shift(a, dx=2)
    got = shift(send, dx=2), shift(give_keep, dcore=1), shift(give_send, dx=2, dcore=1)
    mix = combine(a, a2, b1, b3, keep, *got)
    s0, s1, s2, s3 = (shift(m, dy=d) if d else m for d, m in enumerate(mix))
    out = (s0.astype(f32) + s2.astype(f32)) + (s1.astype(f32) + s3.astype(f32))
    out = out.astype(bf16)
    return out[ROW:].T, out[:ROW].T


def solution(mesh):
    fine = Mesh(mesh.devices.reshape(N_Y, N_XH, N_Z, N_XL, 2), AXES)
    head, ctx = ("y", "xh"), ("z", "xl", "core")
    in_specs = (
        P(ctx, head),
        P(ctx, None),
        P(ctx, head),
        P(None, head),
        P(head, None, None),
        P(head, None, None),
        P(),
    )
    out_specs = (P(ctx, head), P(ctx, None))
    return jax.shard_map(
        per_device, mesh=fine, in_specs=in_specs, out_specs=out_specs, check_vma=False
    )
```

```python
import functools

import jax
import jax.numpy as jnp
import numpy as np
from jax import lax
from jax.experimental import pallas as pl
from jax.experimental.pallas import tpu as pltpu
from jax.sharding import Mesh
from jax.sharding import PartitionSpec as P

D_LAT = 512
D_ROPE = 64
D_NOPE = 128
D_V = 128
BLOCK = 64
ROW = D_LAT + D_ROPE
HALF = D_ROPE // 2
N_Y, N_XH, N_Z, N_XL = 4, 2, 4, 2
N_X = N_XH * N_XL
TOK = 128
HEADS_L = 8
SHARDS = N_Z * N_XL
KEYS = SHARDS * TOK
HROWS = HEADS_L * TOK
ROWS = 2 * HROWS
F_ROWS = HEADS_L * (D_NOPE + D_ROPE)
C_COLS = 192
SCALE = (D_NOPE + D_ROPE) ** -0.5
K_SCALE = SCALE * 1.4426950408889634
MASKED = -1e30
AXES = ("y", "xh", "z", "xl", "core")
TN = 256

SLOTS = ((0, 0), (1, 0), (3, 0), (2, 0), (0, 1), (1, 1), (3, 1), (2, 1))
GROUPS = ((0, 1, 2, 3), (4, 5), (6, 7))

NT = (((1,), (1,)), ((), ()))
NN = (((1,), (0,)), ((), ()))
bf16 = jnp.bfloat16
f32 = jnp.float32


def dot(a, b, dims=NN):
    return lax.dot_general(a, b, dims, preferred_element_type=f32)


def shift(x, dy=0, dx=0, dz=0, dxl=0, dcore=0):
    pairs = []
    for y in range(N_Y):
        for xh in range(N_XH):
            for z in range(N_Z):
                for xl in range(N_XL):
                    for c in range(2):
                        a = (xh * N_XL + xl + dx) % N_X
                        to = ((y + dy) % N_Y) * N_XH + a // N_XL
                        to = to * N_Z + (z + dz) % N_Z
                        to = to * N_XL + (a + dxl) % N_XL
                        to = to * 2 + (c + dcore) % 2
                        pairs.append((len(pairs), to))
    return lax.ppermute(x, AXES, pairs)


def params(mib):
    return pltpu.CompilerParams(vmem_limit_bytes=mib * 1024 * 1024)


def cost(flops, exps=0):
    return pl.CostEstimate(flops=flops, bytes_accessed=1024 * 1024, transcendentals=exps)


def vmem():
    return pl.BlockSpec(memory_space=pltpu.VMEM)


def smem():
    return pl.BlockSpec(memory_space=pltpu.SMEM)


def hbm():
    return pl.BlockSpec(memory_space=pltpu.HBM)


def like(*shape, dtype=bf16):
    return jax.ShapeDtypeStruct(shape, dtype)


def kept(*shape, dtype=bf16):
    return pltpu.VMEM(shape, dtype)


def held(*arrays):
    return [pltpu.with_memory_space_constraint(x, pltpu.VMEM) for x in arrays]


def left(x):
    return pltpu.with_memory_space_constraint(x, pltpu.HBM)


def prologue_kernel(q0, q1, do0, do1, uv_hbm, qt, gt, done, q_own, do_own, uv, sems):
    copies = [
        pltpu.make_async_copy(src, dst, sems.at[i])
        for i, (src, dst) in enumerate(((uv_hbm, uv), (do0, do_own), (q0, q_own)))
    ]
    for c in copies:
        c.start()

    def transpose(s, q):
        for j in range(HEADS_L * ROW // 128):
            t = q[:, j * 128 : (j + 1) * 128].T
            for k in range(2):
                r = j * 128 + k * 64
                h, d = r // ROW, r % ROW
                col = (s * HEADS_L + h) * TOK
                qt[d : d + 64, col : col + TOK] = t[k * 64 : (k + 1) * 64, :]

    def value_grad(s, do):
        for h in range(HEADS_L):
            col = (s * HEADS_L + h) * TOK
            g = dot(uv[h], do[:, h * D_V : (h + 1) * D_V], NT)
            gt[:, col : col + TOK] = g.astype(bf16)

    transpose(1, q1)
    copies[0].wait()
    value_grad(1, do1)
    copies[1].wait()
    value_grad(0, do_own)
    copies[2].wait()
    transpose(0, q_own)
    done[...] = jnp.zeros_like(done)


def prologue(q0, q1, do0, do1, uv):
    return pl.pallas_call(
        prologue_kernel,
        out_shape=(kept(ROW, ROWS), kept(D_LAT, ROWS), like(8, 128, dtype=f32)),
        in_specs=[hbm(), vmem(), hbm(), vmem(), hbm()],
        out_specs=(vmem(),) * 3,
        scratch_shapes=[
            pltpu.VMEM(q0.shape, bf16),
            pltpu.VMEM(do0.shape, bf16),
            pltpu.VMEM(uv.shape, bf16),
            pltpu.SemaphoreType.DMA((3,)),
        ],
        compiler_params=params(10),
        cost_estimate=cost(2 * ROWS * D_V * D_LAT),
        name="prologue",
    )(left(q0), q1, left(do0), do1, left(uv))


def scores_kernel(slots, order, place, qt, gt, *refs):
    n = len(slots)
    kts, refs = refs[:n], refs[n:]
    before = None
    if slots[0]:
        before, refs = refs[0], refs[1:]
    e_out, dp_out, kt_out, m_out, merged, k_nat, bias = refs
    z, xl, core = place[0], place[1], place[2]

    def owner(dz, dxl, c):
        return (lax.rem(z + N_Z - dz, N_Z) * N_XL + lax.rem(xl + dxl, N_XL)) * 2 + c

    lane = lax.broadcasted_iota(jnp.int32, (BLOCK, TOK), 1)
    sub = lax.broadcasted_iota(jnp.int32, (BLOCK, TOK), 0)
    for i, slot in enumerate(slots):
        k_nat[i * TOK : (i + 1) * TOK, :] = kts[i][...].T
        kt_out[:, i * TOK : (i + 1) * TOK] = kts[i][...]
        o = owner(*SLOTS[slot], core)
        for t in range(2):
            q = owner(0, 0, core if t == 0 else 1 - core)
            q_pos = jnp.where(
                lane < BLOCK,
                order[2 * q] * BLOCK + lane,
                order[2 * q + 1] * BLOCK + lane - BLOCK,
            )
            for b in range(2):
                k_pos = order[2 * o + b] * BLOCK + sub
                at = i * TOK + b * BLOCK
                bias[t, at : at + BLOCK, :] = jnp.where(k_pos <= q_pos, 0.0, MASKED)

    for step in range(ROWS // TN):
        base = step * TN
        token_set = step // (HROWS // TN)
        q, g = qt[:, pl.ds(base, TN)], gt[:, pl.ds(base, TN)]
        halves = TN // TOK
        ms, ls, ws = [], [], []
        for i in range(n):
            rows = slice(i * TOK, (i + 1) * TOK)
            sc = dot(k_nat[rows, :], q)
            dp = dot(k_nat[rows, :D_LAT], g)
            b = bias[token_set, rows, :]
            for j in range(halves):
                cols = pl.ds(base + j * TOK, TOK)
                x = sc[:, j * TOK : (j + 1) * TOK] * K_SCALE + b
                m = jnp.max(x, axis=0, keepdims=True)
                e = jnp.exp2(x - m)
                d = dp[:, j * TOK : (j + 1) * TOK]
                ms.append(m)
                ls.append(jnp.sum(e, axis=0, keepdims=True))
                ws.append(jnp.sum(e * d, axis=0, keepdims=True))
                e_out[rows, cols] = e.astype(bf16)
                dp_out[rows, cols] = d.astype(bf16)
                m_out[i : i + 1, cols] = m
        for j in range(halves):
            cols = pl.ds(base + j * TOK, TOK)
            mj, lj, wj = ms[j::halves], ls[j::halves], ws[j::halves]
            if before is not None:
                mj, lj, wj = (
                    a + [before[k : k + 1, cols]] for k, a in enumerate((mj, lj, wj))
                )
            top = functools.reduce(jnp.maximum, mj)
            f = [jnp.exp2(m - top) for m in mj]
            merged[0:1, cols] = top
            merged[1:2, cols] = sum(a * b for a, b in zip(f, lj))
            merged[2:3, cols] = sum(a * b for a, b in zip(f, wj))


def scores(slots, order, place, qt, gt, kts, before=()):
    n = len(slots)
    return pl.pallas_call(
        functools.partial(scores_kernel, slots),
        out_shape=(
            kept(n * TOK, ROWS),
            kept(n * TOK, ROWS),
            kept(ROW, n * TOK),
            like(8, ROWS, dtype=f32),
            like(8, ROWS, dtype=f32),
        ),
        in_specs=[smem(), smem()] + [vmem()] * (2 + n + len(before)),
        out_specs=(vmem(),) * 5,
        scratch_shapes=[pltpu.VMEM((n * TOK, ROW), bf16), pltpu.VMEM((2, n * TOK, TOK), f32)],
        compiler_params=params(8),
        cost_estimate=cost(2 * ROWS * n * TOK * (ROW + D_LAT), ROWS * n * TOK),
        name="scores",
    )(order, place, *held(qt, gt), *kts, *before)


def grads_kernel(counts, *refs):
    n = len(counts)
    es, dps, ms, refs = refs[:n], refs[n : 2 * n], refs[2 * n : 3 * n], refs[3 * n :]
    mine, theirs, qt, gt = refs[:4]
    outs, refs = refs[4 : 4 + N_Z], refs[4 + N_Z :]
    dss, (r_s, rc_s, delta_s, p_s, dk_s, sems) = refs[:n], refs[n:]
    copies = []
    for j in range(2):
        a = slice(j * HROWS, (j + 1) * HROWS)
        b = slice((1 - j) * HROWS, (2 - j) * HROWS)
        m0, m1 = mine[0:1, a], theirs[0:1, b]
        top = jnp.maximum(m0, m1)
        f0, f1 = jnp.exp2(m0 - top), jnp.exp2(m1 - top)
        inv = 1.0 / (f0 * mine[1:2, a] + f1 * theirs[1:2, b])
        delta_s[0:1, a] = (f0 * mine[2:3, a] + f1 * theirs[2:3, b]) * inv
        at = 0
        for m, c in zip(ms, counts):
            r = jnp.exp2(m[:c, a] - top) * inv
            r_s[at : at + c, a] = r
            rc_s[at : at + c, a] = r * SCALE
            at += c
    at = 0
    for e, dp, ds, c in zip(es, dps, dss, counts):
        for k in range(c):
            s = at + k
            rows = slice(k * TOK, (k + 1) * TOK)
            p_rows = slice((s % 4) * TOK, (s % 4 + 1) * TOK)
            for j in range(ROWS // TN):
                cols = slice(j * TN, (j + 1) * TN)
                ef = e[rows, cols].astype(f32)
                p_s[p_rows, cols] = (ef * r_s[s : s + 1, cols]).astype(bf16)
                d = dp[rows, cols].astype(f32) - delta_s[0:1, cols]
                ds[rows, cols] = (ef * rc_s[s : s + 1, cols] * d).astype(bf16)
            if k % 2:
                pair = slice((k - 1) * TOK, (k + 1) * TOK)
                p_pair = slice((s % 4 - 1) * TOK, (s % 4 + 1) * TOK)
                dk = dot(qt[...], ds[pair, :], NT)
                dv = dot(gt[...], p_s[p_pair, :], NT)
                for i in range(2):
                    h = slice(i * TOK, (i + 1) * TOK)
                    o = s - 1 + i
                    dz, dxl = SLOTS[o]
                    dk_s[o, :D_LAT, :] = (dk[:D_LAT, h] + dv[:, h]).astype(bf16)
                    dk_s[o, D_LAT:, :] = dk[D_LAT:, h].astype(bf16)
                    copies.append(pltpu.make_async_copy(dk_s.at[o], outs[dz].at[dxl], sems.at[o]))
                    copies[-1].start()
        at += c
    for copy in copies:
        copy.wait()


def grads(parts, mine, theirs, qt, gt):
    es, dps, ms = zip(*parts)
    counts = tuple(e.shape[0] // TOK for e in es)
    res = pl.pallas_call(
        functools.partial(grads_kernel, counts),
        out_shape=(pltpu.HBM((N_XL, ROW, TOK), bf16),) * N_Z + tuple(kept(*e.shape) for e in es),
        in_specs=[vmem()] * (3 * len(parts) + 4),
        out_specs=(hbm(),) * N_Z + (vmem(),) * len(parts),
        scratch_shapes=[
            pltpu.VMEM((SHARDS, ROWS), f32),
            pltpu.VMEM((SHARDS, ROWS), f32),
            pltpu.VMEM((8, ROWS), f32),
            pltpu.VMEM((4 * TOK, ROWS), bf16),
            pltpu.VMEM((SHARDS, ROW, TOK), bf16),
            pltpu.SemaphoreType.DMA((SHARDS,)),
        ],
        compiler_params=params(8),
        cost_estimate=cost(2 * ROWS * KEYS * (ROW + D_LAT)),
        name="grads",
    )(*held(*es, *dps), *ms, mine, theirs, *held(qt, gt))
    return res[:N_Z], res[N_Z:]


def project_kernel(order, place, uk, uq, frequency, *refs):
    n = (len(refs) - 6) // 2
    lane = lax.broadcasted_iota(jnp.int32, (HALF, TOK), 1)
    dss, kts = refs[:n], refs[n : 2 * n]
    outs, (ft, cg) = refs[2 * n : -2], refs[-2:]
    for t in (1, 0):
        c = place[2] if t == 0 else 1 - place[2]
        at = ((place[0] * N_XL + place[1]) * 2 + c) * 2
        block = jnp.where(lane < BLOCK, order[at], order[at + 1])
        angle = (block * BLOCK + lane % BLOCK).astype(f32) * frequency[...]
        cos, sin = jnp.cos(angle), jnp.sin(angle)
        half = slice(t * HROWS, (t + 1) * HROWS)
        dq = sum(dot(kt[...], ds[:, half]) for kt, ds in zip(kts, dss)).astype(bf16)
        out = slice(t * TOK, (t + 1) * TOK)
        for h in range(HEADS_L):
            d = dq[:, h * TOK : (h + 1) * TOK]
            base = h * (D_NOPE + D_ROPE)
            ft[base : base + D_NOPE, out] = dot(uk[h], d[:D_LAT]).astype(bf16)
            a = d[D_LAT : D_LAT + HALF].astype(f32)
            b = d[D_LAT + HALF :].astype(f32)
            base += D_NOPE
            ft[base : base + HALF, out] = (a * cos + b * sin).astype(bf16)
            ft[base + HALF : base + D_ROPE, out] = (b * cos - a * sin).astype(bf16)
    cg[...] = dot(uq[...], ft[...]).astype(bf16)
    y, xh = place[3], place[4]
    for d in range(N_Y):
        yd = lax.rem(y + d, N_Y)
        for k, h in enumerate((xh, 1 - xh)):
            rows = pl.ds(pl.multiple_of((yd * N_XH + h) * C_COLS, 64), C_COLS)
            for t in range(2):
                outs[d][t, k] = cg[rows, t * TOK : (t + 1) * TOK]


def project(order, place, dss, kts, uk, uq):
    k = np.arange(HALF, dtype=np.float32)[:, None]
    frequency = np.float32(10000.0) ** (-(2.0 * k) / D_ROPE)
    frequency = jnp.asarray(np.broadcast_to(frequency, (HALF, TOK)), f32)
    q_rank = uq.shape[0]
    return pl.pallas_call(
        project_kernel,
        out_shape=(like(2, N_XH, C_COLS, TOK),) * N_Y,
        in_specs=[smem()] * 2 + [vmem()] * (3 + 2 * len(dss)),
        out_specs=(vmem(),) * 4,
        scratch_shapes=[pltpu.VMEM((F_ROWS, 2 * TOK), bf16), pltpu.VMEM((q_rank, 2 * TOK), bf16)],
        compiler_params=params(12),
        cost_estimate=cost(4 * HROWS * KEYS * ROW),
        name="project",
    )(order, place, uk, uq, frequency, *held(*dss, *kts))


def gather_kernel(p0, p1, p2, p3, *outs):
    for t in range(2):
        for k in range(N_XH):
            a, b, c, d = (p[t, k].astype(f32) for p in (p0, p1, p2, p3))
            outs[2 * t + k][...] = ((a + c) + (b + d)).astype(bf16)


def gather(*parts):
    return pl.pallas_call(
        gather_kernel,
        out_shape=(like(C_COLS, TOK),) * 4,
        in_specs=[vmem()] * N_Y,
        out_specs=(vmem(),) * 4,
        compiler_params=params(4),
        cost_estimate=cost(0),
        name="gather",
    )(*parts)


def add(*parts):
    return sum(p.astype(f32) for p in parts).astype(bf16)


def per_device(queries, latent_rows, output_grad, up_query, up_key, up_value, block_order):
    coords = [lax.axis_index(a) for a in ("z", "xl", "core", "y", "xh")]
    place = jnp.stack(coords).astype(jnp.int32)

    own = latent_rows.T
    q_other = shift(queries, dcore=1)
    do_other = shift(output_grad, dcore=1)
    kts = [own] + [shift(own, dz=dz) for dz, _ in SLOTS[1:N_Z]]
    qt, gt, done = prologue(queries, q_other, output_grad, do_other, up_value)
    for i, dx in enumerate((1, 3, 1, 3)):
        kt = lax.optimization_barrier((kts[i], done))[0] if i else kts[0]
        kts.append(shift(kt, dx=dx))

    parts, kt_parts, mine = [], [], ()
    for slots in GROUPS:
        took = kts[slots[0] : slots[-1] + 1]
        e, dp, kt, m, mine = scores(slots, block_order, place, qt, gt, took, mine)
        parts.append((e, dp, m))
        kt_parts.append(kt)
        mine = (mine,)
    mine = mine[0]
    theirs = shift(mine, dcore=1)
    dk, dss = grads(parts, mine, theirs, qt, gt)

    from_z = [shift(dk[dz], dz=-dz) for dz in range(1, N_Z)]
    a, b = (add(*(p[i] for p in (dk[0], *from_z))) for i in range(N_XL))

    cg = project(block_order, place, dss, kt_parts, up_key, up_query)

    b1, b3, a2 = shift(b, dx=1), shift(b, dx=3), shift(a, dx=2)
    total = ((a.astype(f32) + a2.astype(f32)) + (b1.astype(f32) + b3.astype(f32))).astype(bf16)
    s1, s2, s3 = (shift(total, dy=d).astype(f32) for d in range(1, N_Y))
    total = ((total.astype(f32) + s2) + (s1 + s3)).astype(bf16)

    keep, send, give_keep, give_send = gather(cg[0], *(shift(cg[d], dy=d) for d in range(1, N_Y)))
    got = shift(send, dx=2), shift(give_keep, dcore=1), shift(give_send, dx=2, dcore=1)
    return add(keep, *got).T, total.T


def solution(mesh):
    fine = Mesh(mesh.devices.reshape(N_Y, N_XH, N_Z, N_XL, 2), AXES)
    head, ctx = ("y", "xh"), ("z", "xl", "core")
    in_specs = (
        P(ctx, head),
        P(ctx, None),
        P(ctx, head),
        P(None, head),
        P(head, None, None),
        P(head, None, None),
        P(),
    )
    out_specs = (P(ctx, head), P(ctx, None))
    return jax.shard_map(
        per_device, mesh=fine, in_specs=in_specs, out_specs=out_specs, check_vma=False
    )
```

```python
import functools

import jax
import jax.numpy as jnp
import numpy as np
from jax import lax
from jax.experimental import pallas as pl
from jax.experimental.pallas import tpu as pltpu
from jax.sharding import Mesh
from jax.sharding import PartitionSpec as P

D_LAT = 512
D_ROPE = 64
D_NOPE = 128
D_V = 128
BLOCK = 64
ROW = D_LAT + D_ROPE
HALF = D_ROPE // 2
N_Y, N_XH, N_Z, N_XL = 4, 2, 4, 2
N_X = N_XH * N_XL
TOK = 128
HEADS_L = 8
SHARDS = N_Z * N_XL
KEYS = SHARDS * TOK
HROWS = HEADS_L * TOK
ROWS = 2 * HROWS
F_ROWS = HEADS_L * (D_NOPE + D_ROPE)
C_COLS = 192
SCALE = (D_NOPE + D_ROPE) ** -0.5
K_SCALE = SCALE * 1.4426950408889634
MASKED = -1e30
AXES = ("y", "xh", "z", "xl", "core")
TN = 256

SLOTS = ((1, 0), (3, 0), (0, 0), (2, 0), (1, 1), (3, 1), (0, 1), (2, 1))
GROUPS = ((0, 1, 2, 3), (4, 5), (6, 7))

NT = (((1,), (1,)), ((), ()))
NN = (((1,), (0,)), ((), ()))
bf16 = jnp.bfloat16
f32 = jnp.float32


def dot(a, b, dims=NN):
    return lax.dot_general(a, b, dims, preferred_element_type=f32)


def shift(x, dy=0, dx=0, dz=0, dxl=0, dcore=0):
    pairs = []
    for y in range(N_Y):
        for xh in range(N_XH):
            for z in range(N_Z):
                for xl in range(N_XL):
                    for c in range(2):
                        a = (xh * N_XL + xl + dx) % N_X
                        to = ((y + dy) % N_Y) * N_XH + a // N_XL
                        to = to * N_Z + (z + dz) % N_Z
                        to = to * N_XL + (a + dxl) % N_XL
                        to = to * 2 + (c + dcore) % 2
                        pairs.append((len(pairs), to))
    return lax.ppermute(x, AXES, pairs)


def params(mib):
    return pltpu.CompilerParams(vmem_limit_bytes=mib * 1024 * 1024)


def cost(flops, exps=0):
    return pl.CostEstimate(flops=flops, bytes_accessed=1024 * 1024, transcendentals=exps)


def vmem():
    return pl.BlockSpec(memory_space=pltpu.VMEM)


def smem():
    return pl.BlockSpec(memory_space=pltpu.SMEM)


def hbm():
    return pl.BlockSpec(memory_space=pltpu.HBM)


def like(*shape, dtype=bf16):
    return jax.ShapeDtypeStruct(shape, dtype)


def kept(*shape, dtype=bf16):
    return pltpu.VMEM(shape, dtype)


def held(*arrays):
    return [pltpu.with_memory_space_constraint(x, pltpu.VMEM) for x in arrays]


def left(x):
    return pltpu.with_memory_space_constraint(x, pltpu.HBM)


def prologue_kernel(q0, q1, do0, do1, uv_hbm, qt, gt, done, q_own, do_own, uv, sems):
    copies = [
        pltpu.make_async_copy(src, dst, sems.at[i])
        for i, (src, dst) in enumerate(((uv_hbm, uv), (do0, do_own), (q0, q_own)))
    ]
    for c in copies:
        c.start()

    def transpose(s, q):
        for j in range(HEADS_L * ROW // 128):
            t = q[:, j * 128 : (j + 1) * 128].T
            for k in range(2):
                r = j * 128 + k * 64
                h, d = r // ROW, r % ROW
                col = (s * HEADS_L + h) * TOK
                qt[d : d + 64, col : col + TOK] = t[k * 64 : (k + 1) * 64, :]

    def value_grad(s, do):
        for h in range(HEADS_L):
            col = (s * HEADS_L + h) * TOK
            g = dot(uv[h], do[:, h * D_V : (h + 1) * D_V], NT)
            gt[:, col : col + TOK] = g.astype(bf16)

    transpose(1, q1)
    copies[0].wait()
    value_grad(1, do1)
    copies[1].wait()
    value_grad(0, do_own)
    copies[2].wait()
    transpose(0, q_own)
    done[...] = jnp.zeros_like(done)


def prologue(q0, q1, do0, do1, uv):
    return pl.pallas_call(
        prologue_kernel,
        out_shape=(kept(ROW, ROWS), kept(D_LAT, ROWS), like(8, 128, dtype=f32)),
        in_specs=[hbm(), vmem(), hbm(), vmem(), hbm()],
        out_specs=(vmem(),) * 3,
        scratch_shapes=[
            pltpu.VMEM(q0.shape, bf16),
            pltpu.VMEM(do0.shape, bf16),
            pltpu.VMEM(uv.shape, bf16),
            pltpu.SemaphoreType.DMA((3,)),
        ],
        compiler_params=params(10),
        cost_estimate=cost(2 * ROWS * D_V * D_LAT),
        name="prologue",
    )(left(q0), q1, left(do0), do1, left(uv))


def scores_kernel(slots, order, place, qt, gt, *refs):
    n = len(slots)
    kts, refs = refs[:n], refs[n:]
    before = None
    if slots[0]:
        before, refs = refs[0], refs[1:]
    e_out, dp_out, kt_out, m_out, merged, k_nat, bias = refs
    z, xl, core = place[0], place[1], place[2]

    def owner(dz, dxl, c):
        return (lax.rem(z + N_Z - dz, N_Z) * N_XL + lax.rem(xl + dxl, N_XL)) * 2 + c

    lane = lax.broadcasted_iota(jnp.int32, (BLOCK, TOK), 1)
    sub = lax.broadcasted_iota(jnp.int32, (BLOCK, TOK), 0)
    for i, slot in enumerate(slots):
        k_nat[i * TOK : (i + 1) * TOK, :] = kts[i][...].T
        kt_out[:, i * TOK : (i + 1) * TOK] = kts[i][...]
        o = owner(*SLOTS[slot], core)
        for t in range(2):
            q = owner(0, 0, core if t == 0 else 1 - core)
            q_pos = jnp.where(
                lane < BLOCK,
                order[2 * q] * BLOCK + lane,
                order[2 * q + 1] * BLOCK + lane - BLOCK,
            )
            for b in range(2):
                k_pos = order[2 * o + b] * BLOCK + sub
                at = i * TOK + b * BLOCK
                bias[t, at : at + BLOCK, :] = jnp.where(k_pos <= q_pos, 0.0, MASKED)

    for step in range(ROWS // TN):
        base = step * TN
        token_set = step // (HROWS // TN)
        q, g = qt[:, pl.ds(base, TN)], gt[:, pl.ds(base, TN)]
        halves = TN // TOK
        ms, ls, ws = [], [], []
        for i in range(n):
            rows = slice(i * TOK, (i + 1) * TOK)
            sc = dot(k_nat[rows, :], q)
            dp = dot(k_nat[rows, :D_LAT], g)
            b = bias[token_set, rows, :]
            for j in range(halves):
                cols = pl.ds(base + j * TOK, TOK)
                x = sc[:, j * TOK : (j + 1) * TOK] * K_SCALE + b
                m = jnp.max(x, axis=0, keepdims=True)
                e = jnp.exp2(x - m)
                d = dp[:, j * TOK : (j + 1) * TOK]
                ms.append(m)
                ls.append(jnp.sum(e, axis=0, keepdims=True))
                ws.append(jnp.sum(e * d, axis=0, keepdims=True))
                e_out[rows, cols] = e.astype(bf16)
                dp_out[rows, cols] = d.astype(bf16)
                m_out[i : i + 1, cols] = m
        for j in range(halves):
            cols = pl.ds(base + j * TOK, TOK)
            mj, lj, wj = ms[j::halves], ls[j::halves], ws[j::halves]
            if before is not None:
                mj, lj, wj = (
                    a + [before[k : k + 1, cols]] for k, a in enumerate((mj, lj, wj))
                )
            top = functools.reduce(jnp.maximum, mj)
            f = [jnp.exp2(m - top) for m in mj]
            merged[0:1, cols] = top
            merged[1:2, cols] = sum(a * b for a, b in zip(f, lj))
            merged[2:3, cols] = sum(a * b for a, b in zip(f, wj))


def scores(slots, order, place, qt, gt, kts, before=()):
    n = len(slots)
    return pl.pallas_call(
        functools.partial(scores_kernel, slots),
        out_shape=(
            kept(n * TOK, ROWS),
            kept(n * TOK, ROWS),
            kept(ROW, n * TOK),
            like(8, ROWS, dtype=f32),
            like(8, ROWS, dtype=f32),
        ),
        in_specs=[smem(), smem()] + [vmem()] * (2 + n + len(before)),
        out_specs=(vmem(),) * 5,
        scratch_shapes=[pltpu.VMEM((n * TOK, ROW), bf16), pltpu.VMEM((2, n * TOK, TOK), f32)],
        compiler_params=params(8),
        cost_estimate=cost(2 * ROWS * n * TOK * (ROW + D_LAT), ROWS * n * TOK),
        name="scores",
    )(order, place, *held(qt, gt), *kts, *before)


def grads_kernel(picks, *refs):
    n = len(picks)
    es, dps, ms, refs = refs[:n], refs[n : 2 * n], refs[2 * n : 3 * n], refs[3 * n :]
    mine, theirs, qt, gt = refs[:4]
    outs, dss, (r_s, rc_s, delta_s, p_s) = refs[4:6], refs[6 : 6 + n], refs[6 + n :]
    for j in range(2):
        a = slice(j * HROWS, (j + 1) * HROWS)
        b = slice((1 - j) * HROWS, (2 - j) * HROWS)
        m0, m1 = mine[0:1, a], theirs[0:1, b]
        top = jnp.maximum(m0, m1)
        f0, f1 = jnp.exp2(m0 - top), jnp.exp2(m1 - top)
        inv = 1.0 / (f0 * mine[1:2, a] + f1 * theirs[1:2, b])
        delta_s[0:1, a] = (f0 * mine[2:3, a] + f1 * theirs[2:3, b]) * inv
        for i, (m, at) in enumerate(zip(ms, picks)):
            r = jnp.exp2(m[at : at + 2, a] - top) * inv
            r_s[2 * i : 2 * i + 2, a] = r
            rc_s[2 * i : 2 * i + 2, a] = r * SCALE
    for i, (e, dp, ds, at) in enumerate(zip(es, dps, dss, picks)):
        for k in range(2):
            s = 2 * i + k
            rows = slice((at + k) * TOK, (at + k + 1) * TOK)
            to = slice(k * TOK, (k + 1) * TOK)
            p_to = slice(s * TOK, (s + 1) * TOK)
            for j in range(ROWS // TN):
                cols = slice(j * TN, (j + 1) * TN)
                ef = e[rows, cols].astype(f32)
                p_s[p_to, cols] = (ef * r_s[s : s + 1, cols]).astype(bf16)
                d = dp[rows, cols].astype(f32) - delta_s[0:1, cols]
                ds[to, cols] = (ef * rc_s[s : s + 1, cols] * d).astype(bf16)
        dk = dot(qt[...], ds[...], NT)
        dv = dot(gt[...], p_s[2 * i * TOK : (2 * i + 2) * TOK, :], NT)
        for k in range(2):
            h = slice(k * TOK, (k + 1) * TOK)
            outs[k][i, :D_LAT, :] = (dk[:D_LAT, h] + dv[:, h]).astype(bf16)
            outs[k][i, D_LAT:, :] = dk[D_LAT:, h].astype(bf16)


def grads(parts, mine, theirs, qt, gt):
    es, dps, ms, picks = zip(*parts)
    n = len(parts)
    res = pl.pallas_call(
        functools.partial(grads_kernel, picks),
        out_shape=(like(N_XL, ROW, TOK),) * 2 + (kept(2 * TOK, ROWS),) * n,
        in_specs=[vmem()] * (3 * n + 4),
        out_specs=(vmem(),) * (2 + n),
        scratch_shapes=[
            pltpu.VMEM((8, ROWS), f32),
            pltpu.VMEM((8, ROWS), f32),
            pltpu.VMEM((8, ROWS), f32),
            pltpu.VMEM((2 * n * TOK, ROWS), bf16),
        ],
        compiler_params=params(8),
        cost_estimate=cost(2 * ROWS * n * 2 * TOK * (ROW + D_LAT)),
        name="grads",
    )(*held(*es, *dps), *ms, mine, theirs, *held(qt, gt))
    return res[:2], res[2:]


def project_kernel(order, place, uk, uq, frequency, *refs):
    dss, (near, far0, far1), refs = refs[:N_Z], refs[N_Z : N_Z + 3], refs[N_Z + 3 :]
    kts = near[:, : 2 * TOK], far0[...], near[:, 2 * TOK :], far1[...]
    outs, (ft, cg) = refs[:N_Y], refs[N_Y:]
    lane = lax.broadcasted_iota(jnp.int32, (HALF, TOK), 1)
    angles, dqs = [], []
    for t in range(2):
        c = place[2] if t == 0 else 1 - place[2]
        at = ((place[0] * N_XL + place[1]) * 2 + c) * 2
        block = jnp.where(lane < BLOCK, order[at], order[at + 1])
        angles.append((block * BLOCK + lane % BLOCK).astype(f32) * frequency[...])
        half = slice(t * HROWS, (t + 1) * HROWS)
        dqs.append(sum(dot(kt, ds[:, half]) for kt, ds in zip(kts, dss)).astype(bf16))
    angle = jnp.concatenate(angles, axis=1)
    cos, sin = jnp.cos(angle), jnp.sin(angle)
    for h in range(HEADS_L):
        d = jnp.concatenate([dq[:, h * TOK : (h + 1) * TOK] for dq in dqs], axis=1)
        base = h * (D_NOPE + D_ROPE)
        ft[base : base + D_NOPE, :] = dot(uk[h], d[:D_LAT]).astype(bf16)
        a = d[D_LAT : D_LAT + HALF].astype(f32)
        b = d[D_LAT + HALF :].astype(f32)
        base += D_NOPE
        ft[base : base + HALF, :] = (a * cos + b * sin).astype(bf16)
        ft[base + HALF : base + D_ROPE, :] = (b * cos - a * sin).astype(bf16)
    cg[...] = dot(uq[...], ft[...]).astype(bf16)
    y, xh = place[3], place[4]
    for d in range(N_Y):
        yd = lax.rem(y + d, N_Y)
        for k, h in enumerate((xh, 1 - xh)):
            rows = pl.ds(pl.multiple_of((yd * N_XH + h) * C_COLS, 64), C_COLS)
            for t in range(2):
                outs[d][t, k] = cg[rows, t * TOK : (t + 1) * TOK]


def project(order, place, dss, kts, uk, uq):
    k = np.arange(HALF, dtype=np.float32)[:, None]
    frequency = np.float32(10000.0) ** (-(2.0 * k) / D_ROPE)
    frequency = jnp.asarray(np.broadcast_to(frequency, (HALF, TOK)), f32)
    q_rank = uq.shape[0]
    return pl.pallas_call(
        project_kernel,
        out_shape=(like(2, N_XH, C_COLS, TOK),) * N_Y,
        in_specs=[smem()] * 2 + [vmem()] * (3 + len(dss) + len(kts)),
        out_specs=(vmem(),) * 4,
        scratch_shapes=[pltpu.VMEM((F_ROWS, 2 * TOK), bf16), pltpu.VMEM((q_rank, 2 * TOK), bf16)],
        compiler_params=params(12),
        cost_estimate=cost(4 * HROWS * KEYS * ROW),
        name="project",
    )(order, place, uk, uq, frequency, *held(*dss, *kts))


def gather_kernel(p0, p1, p2, p3, *outs):
    for t in range(2):
        for k in range(N_XH):
            a, b, d, c = (p[t, k].astype(f32) for p in (p0, p1, p2, p3))
            outs[2 * t + k][...] = ((a + c) + (b + d)).astype(bf16)


def gather(*parts):
    return pl.pallas_call(
        gather_kernel,
        out_shape=(like(C_COLS, TOK),) * 4,
        in_specs=[vmem()] * N_Y,
        out_specs=(vmem(),) * 4,
        compiler_params=params(4),
        cost_estimate=cost(0),
        name="gather",
    )(*parts)


def add(*parts):
    return sum(p.astype(f32) for p in parts).astype(bf16)


def per_device(queries, latent_rows, output_grad, up_query, up_key, up_value, block_order):
    coords = [lax.axis_index(a) for a in ("z", "xl", "core", "y", "xh")]
    place = jnp.stack(coords).astype(jnp.int32)

    own = latent_rows.T
    q_other = shift(queries, dcore=1)
    do_other = shift(output_grad, dcore=1)
    kts = [shift(own, dz=dz) if dz else own for dz, _ in SLOTS[:N_Z]]
    qt, gt, done = prologue(queries, q_other, output_grad, do_other, up_value)
    for (dz, _), kt, dx in zip(SLOTS, kts[:], (1, 3, 1, 3)):
        kt = lax.optimization_barrier((kt, done))[0] if dz else kt
        kts.append(shift(kt, dx=dx))

    parts, kt_parts, mine = [], [], ()
    for slots in GROUPS:
        took = kts[slots[0] : slots[-1] + 1]
        e, dp, kt, m, mine = scores(slots, block_order, place, qt, gt, took, mine)
        parts.append((e, dp, m))
        kt_parts.append(kt)
        mine = (mine,)
    mine = mine[0]
    theirs = shift(mine, dcore=1)
    near, far0, far1 = parts
    (dk1, dk3), dss = grads([(*near, 0), (*far0, 0)], mine, theirs, qt, gt)
    (dk0, dk2), more = grads([(*near, 2), (*far1, 0)], mine, theirs, qt, gt)
    dss = *dss, *more

    from_z = [shift(dk, dz=-dz) for dz, dk in ((1, dk1), (3, dk3), (2, dk2))]
    a, b = (add(*(p[i] for p in (dk0, *from_z))) for i in range(N_XL))

    cg = project(block_order, place, dss, kt_parts, up_key, up_query)

    b1, b3, a2 = shift(b, dx=1), shift(b, dx=3), shift(a, dx=2)
    total = ((a.astype(f32) + a2.astype(f32)) + (b1.astype(f32) + b3.astype(f32))).astype(bf16)
    s1, s3, s2 = (shift(total, dy=d).astype(f32) for d in (1, 3, 2))
    total = ((total.astype(f32) + s2) + (s1 + s3)).astype(bf16)

    keep, send, give_keep, give_send = gather(cg[0], *(shift(cg[d], dy=d) for d in (1, 3, 2)))
    got = shift(send, dx=2), shift(give_keep, dcore=1), shift(give_send, dx=2, dcore=1)
    return add(keep, *got).T, total.T


def solution(mesh):
    fine = Mesh(mesh.devices.reshape(N_Y, N_XH, N_Z, N_XL, 2), AXES)
    head, ctx = ("y", "xh"), ("z", "xl", "core")
    in_specs = (
        P(ctx, head),
        P(ctx, None),
        P(ctx, head),
        P(None, head),
        P(head, None, None),
        P(head, None, None),
        P(),
    )
    out_specs = (P(ctx, head), P(ctx, None))
    return jax.shard_map(
        per_device, mesh=fine, in_specs=in_specs, out_specs=out_specs, check_vma=False
    )
```

```python
import functools

import jax
import jax.numpy as jnp
import numpy as np
from jax import lax
from jax.experimental import pallas as pl
from jax.experimental.pallas import tpu as pltpu
from jax.sharding import Mesh
from jax.sharding import PartitionSpec as P

D_LAT = 512
D_ROPE = 64
D_NOPE = 128
D_V = 128
BLOCK = 64
ROW = D_LAT + D_ROPE
HALF = D_ROPE // 2
N_Y, N_XH, N_Z, N_XL = 4, 2, 4, 2
N_X = N_XH * N_XL
TOK = 128
HEADS_L = 8
SHARDS = N_Z * N_XL
KEYS = SHARDS * TOK
HROWS = HEADS_L * TOK
ROWS = 2 * HROWS
F_ROWS = HEADS_L * (D_NOPE + D_ROPE)
C_COLS = 192
SCALE = (D_NOPE + D_ROPE) ** -0.5
K_SCALE = SCALE * 1.4426950408889634
MASKED = -1e30
AXES = ("y", "xh", "z", "xl", "core")
TN = 256
CUTS = 4

SLOTS = ((1, 0), (3, 0), (0, 0), (2, 0), (1, 1), (3, 1), (0, 1), (2, 1))
GROUPS = ((0, 1, 2, 3), (4, 5), (6, 7))

NT = (((1,), (1,)), ((), ()))
NN = (((1,), (0,)), ((), ()))
bf16 = jnp.bfloat16
f32 = jnp.float32


def dot(a, b, dims=NN):
    return lax.dot_general(a, b, dims, preferred_element_type=f32)


def shift(x, dy=0, dx=0, dz=0, dxl=0, dcore=0):
    pairs = []
    for y in range(N_Y):
        for xh in range(N_XH):
            for z in range(N_Z):
                for xl in range(N_XL):
                    for c in range(2):
                        a = (xh * N_XL + xl + dx) % N_X
                        to = ((y + dy) % N_Y) * N_XH + a // N_XL
                        to = to * N_Z + (z + dz) % N_Z
                        to = to * N_XL + (a + dxl) % N_XL
                        to = to * 2 + (c + dcore) % 2
                        pairs.append((len(pairs), to))
    return lax.ppermute(x, AXES, pairs)


def params(mib):
    return pltpu.CompilerParams(vmem_limit_bytes=mib * 1024 * 1024)


def cost(flops, exps=0):
    return pl.CostEstimate(flops=flops, bytes_accessed=1024 * 1024, transcendentals=exps)


def vmem():
    return pl.BlockSpec(memory_space=pltpu.VMEM)


def smem():
    return pl.BlockSpec(memory_space=pltpu.SMEM)


def hbm():
    return pl.BlockSpec(memory_space=pltpu.HBM)


def like(*shape, dtype=bf16):
    return jax.ShapeDtypeStruct(shape, dtype)


def kept(*shape, dtype=bf16):
    return pltpu.VMEM(shape, dtype)


def held(*arrays):
    return [pltpu.with_memory_space_constraint(x, pltpu.VMEM) for x in arrays]


def left(x):
    return pltpu.with_memory_space_constraint(x, pltpu.HBM)


def prologue_kernel(q0, q1, do0, do1, uv_hbm, qt, gt, done, q_own, do_own, uv, sems):
    copies = []
    for i, (src, dst) in enumerate(((uv_hbm, uv), (do0, do_own), (q0, q_own))):
        part = src.shape[0] // CUTS
        for k in range(CUTS):
            rows = pl.ds(k * part, part)
            copies.append(pltpu.make_async_copy(src.at[rows], dst.at[rows], sems.at[i, k]))
            copies[-1].start()

    def wait(i):
        for c in copies[i * CUTS : (i + 1) * CUTS]:
            c.wait()

    def transpose(s, q):
        for j in range(HEADS_L * ROW // 128):
            t = q[:, j * 128 : (j + 1) * 128].T
            for k in range(2):
                r = j * 128 + k * 64
                h, d = r // ROW, r % ROW
                col = (s * HEADS_L + h) * TOK
                qt[d : d + 64, col : col + TOK] = t[k * 64 : (k + 1) * 64, :]

    def value_grad(s, do):
        for h in range(HEADS_L):
            col = (s * HEADS_L + h) * TOK
            g = dot(uv[h], do[:, h * D_V : (h + 1) * D_V], NT)
            gt[:, col : col + TOK] = g.astype(bf16)

    transpose(1, q1)
    wait(0)
    value_grad(1, do1)
    wait(1)
    value_grad(0, do_own)
    wait(2)
    transpose(0, q_own)
    done[...] = jnp.zeros_like(done)


def prologue(q0, q1, do0, do1, uv):
    return pl.pallas_call(
        prologue_kernel,
        out_shape=(kept(ROW, ROWS), kept(D_LAT, ROWS), like(8, 128, dtype=f32)),
        in_specs=[hbm(), vmem(), hbm(), vmem(), hbm()],
        out_specs=(vmem(),) * 3,
        scratch_shapes=[
            pltpu.VMEM(q0.shape, bf16),
            pltpu.VMEM(do0.shape, bf16),
            pltpu.VMEM(uv.shape, bf16),
            pltpu.SemaphoreType.DMA((3, CUTS)),
        ],
        compiler_params=params(10),
        cost_estimate=cost(2 * ROWS * D_V * D_LAT),
        name="prologue",
    )(left(q0), q1, left(do0), do1, left(uv))


def scores_kernel(slots, order, place, qt, gt, *refs):
    n = len(slots)
    kts, refs = refs[:n], refs[n:]
    before = None
    if slots[0]:
        before, refs = refs[0], refs[1:]
    e_out, dp_out, kt_out, m_out, merged, k_nat, bias = refs
    z, xl, core = place[0], place[1], place[2]

    def owner(dz, dxl, c):
        return (lax.rem(z + N_Z - dz, N_Z) * N_XL + lax.rem(xl + dxl, N_XL)) * 2 + c

    lane = lax.broadcasted_iota(jnp.int32, (BLOCK, TOK), 1)
    sub = lax.broadcasted_iota(jnp.int32, (BLOCK, TOK), 0)
    for i, slot in enumerate(slots):
        k_nat[i * TOK : (i + 1) * TOK, :] = kts[i][...].T
        kt_out[:, i * TOK : (i + 1) * TOK] = kts[i][...]
        o = owner(*SLOTS[slot], core)
        for t in range(2):
            q = owner(0, 0, core if t == 0 else 1 - core)
            q_pos = jnp.where(
                lane < BLOCK,
                order[2 * q] * BLOCK + lane,
                order[2 * q + 1] * BLOCK + lane - BLOCK,
            )
            for b in range(2):
                k_pos = order[2 * o + b] * BLOCK + sub
                at = i * TOK + b * BLOCK
                bias[t, at : at + BLOCK, :] = jnp.where(k_pos <= q_pos, 0.0, MASKED)

    for step in range(ROWS // TN):
        base = step * TN
        token_set = step // (HROWS // TN)
        q, g = qt[:, pl.ds(base, TN)], gt[:, pl.ds(base, TN)]
        halves = TN // TOK
        ms, ls, ws = [], [], []
        for i in range(n):
            rows = slice(i * TOK, (i + 1) * TOK)
            sc = dot(k_nat[rows, :], q)
            dp = dot(k_nat[rows, :D_LAT], g)
            b = bias[token_set, rows, :]
            for j in range(halves):
                cols = pl.ds(base + j * TOK, TOK)
                x = sc[:, j * TOK : (j + 1) * TOK] * K_SCALE + b
                m = jnp.max(x, axis=0, keepdims=True)
                e = jnp.exp2(x - m)
                d = dp[:, j * TOK : (j + 1) * TOK]
                ms.append(m)
                ls.append(jnp.sum(e, axis=0, keepdims=True))
                ws.append(jnp.sum(e * d, axis=0, keepdims=True))
                e_out[rows, cols] = e.astype(bf16)
                dp_out[rows, cols] = d.astype(bf16)
                m_out[i : i + 1, cols] = m
        for j in range(halves):
            cols = pl.ds(base + j * TOK, TOK)
            mj, lj, wj = ms[j::halves], ls[j::halves], ws[j::halves]
            if before is not None:
                mj, lj, wj = (
                    a + [before[k : k + 1, cols]] for k, a in enumerate((mj, lj, wj))
                )
            top = functools.reduce(jnp.maximum, mj)
            f = [jnp.exp2(m - top) for m in mj]
            merged[0:1, cols] = top
            merged[1:2, cols] = sum(a * b for a, b in zip(f, lj))
            merged[2:3, cols] = sum(a * b for a, b in zip(f, wj))


def scores(slots, order, place, qt, gt, kts, before=()):
    n = len(slots)
    return pl.pallas_call(
        functools.partial(scores_kernel, slots),
        out_shape=(
            kept(n * TOK, ROWS),
            kept(n * TOK, ROWS),
            kept(ROW, n * TOK),
            like(8, ROWS, dtype=f32),
            like(8, ROWS, dtype=f32),
        ),
        in_specs=[smem(), smem()] + [vmem()] * (2 + n + len(before)),
        out_specs=(vmem(),) * 5,
        scratch_shapes=[pltpu.VMEM((n * TOK, ROW), bf16), pltpu.VMEM((2, n * TOK, TOK), f32)],
        compiler_params=params(8),
        cost_estimate=cost(2 * ROWS * n * TOK * (ROW + D_LAT), ROWS * n * TOK),
        name="scores",
    )(order, place, *held(qt, gt), *kts, *before)


def grads_kernel(picks, *refs):
    n = len(picks)
    es, dps, ms, refs = refs[:n], refs[n : 2 * n], refs[2 * n : 3 * n], refs[3 * n :]
    mine, theirs, qt, gt = refs[:4]
    outs, dss, (r_s, rc_s, delta_s, p_s) = refs[4:6], refs[6 : 6 + n], refs[6 + n :]
    for j in range(2):
        a = slice(j * HROWS, (j + 1) * HROWS)
        b = slice((1 - j) * HROWS, (2 - j) * HROWS)
        m0, m1 = mine[0:1, a], theirs[0:1, b]
        top = jnp.maximum(m0, m1)
        f0, f1 = jnp.exp2(m0 - top), jnp.exp2(m1 - top)
        inv = 1.0 / (f0 * mine[1:2, a] + f1 * theirs[1:2, b])
        delta_s[0:1, a] = (f0 * mine[2:3, a] + f1 * theirs[2:3, b]) * inv
        for i, (m, at) in enumerate(zip(ms, picks)):
            r = jnp.exp2(m[at : at + 2, a] - top) * inv
            r_s[2 * i : 2 * i + 2, a] = r
            rc_s[2 * i : 2 * i + 2, a] = r * SCALE
    for i, (e, dp, ds, at) in enumerate(zip(es, dps, dss, picks)):
        for k in range(2):
            s = 2 * i + k
            rows = slice((at + k) * TOK, (at + k + 1) * TOK)
            to = slice(k * TOK, (k + 1) * TOK)
            p_to = slice(s * TOK, (s + 1) * TOK)
            for j in range(ROWS // TN):
                cols = slice(j * TN, (j + 1) * TN)
                ef = e[rows, cols].astype(f32)
                p_s[p_to, cols] = (ef * r_s[s : s + 1, cols]).astype(bf16)
                d = dp[rows, cols].astype(f32) - delta_s[0:1, cols]
                ds[to, cols] = (ef * rc_s[s : s + 1, cols] * d).astype(bf16)
        dk = dot(qt[...], ds[...], NT)
        dv = dot(gt[...], p_s[2 * i * TOK : (2 * i + 2) * TOK, :], NT)
        for k in range(2):
            h = slice(k * TOK, (k + 1) * TOK)
            outs[k][i, :D_LAT, :] = (dk[:D_LAT, h] + dv[:, h]).astype(bf16)
            outs[k][i, D_LAT:, :] = dk[D_LAT:, h].astype(bf16)


def grads(parts, mine, theirs, qt, gt):
    es, dps, ms, picks = zip(*parts)
    n = len(parts)
    res = pl.pallas_call(
        functools.partial(grads_kernel, picks),
        out_shape=(like(N_XL, ROW, TOK),) * 2 + (kept(2 * TOK, ROWS),) * n,
        in_specs=[vmem()] * (3 * n + 4),
        out_specs=(vmem(),) * (2 + n),
        scratch_shapes=[
            pltpu.VMEM((8, ROWS), f32),
            pltpu.VMEM((8, ROWS), f32),
            pltpu.VMEM((8, ROWS), f32),
            pltpu.VMEM((2 * n * TOK, ROWS), bf16),
        ],
        compiler_params=params(8),
        cost_estimate=cost(2 * ROWS * n * 2 * TOK * (ROW + D_LAT)),
        name="grads",
    )(*held(*es, *dps), *ms, mine, theirs, *held(qt, gt))
    return res[:2], res[2:]


def project_kernel(order, place, uk, uq, frequency, *refs):
    dss, (near, far0, far1), refs = refs[:N_Z], refs[N_Z : N_Z + 3], refs[N_Z + 3 :]
    kts = near[:, : 2 * TOK], far0[...], near[:, 2 * TOK :], far1[...]
    outs, (ft, cg) = refs[:N_Y], refs[N_Y:]
    lane = lax.broadcasted_iota(jnp.int32, (HALF, TOK), 1)
    angles, dqs = [], []
    for t in range(2):
        c = place[2] if t == 0 else 1 - place[2]
        at = ((place[0] * N_XL + place[1]) * 2 + c) * 2
        block = jnp.where(lane < BLOCK, order[at], order[at + 1])
        angles.append((block * BLOCK + lane % BLOCK).astype(f32) * frequency[...])
        half = slice(t * HROWS, (t + 1) * HROWS)
        dqs.append(sum(dot(kt, ds[:, half]) for kt, ds in zip(kts, dss)).astype(bf16))
    angle = jnp.concatenate(angles, axis=1)
    cos, sin = jnp.cos(angle), jnp.sin(angle)
    for h in range(HEADS_L):
        d = jnp.concatenate([dq[:, h * TOK : (h + 1) * TOK] for dq in dqs], axis=1)
        base = h * (D_NOPE + D_ROPE)
        ft[base : base + D_NOPE, :] = dot(uk[h], d[:D_LAT]).astype(bf16)
        a = d[D_LAT : D_LAT + HALF].astype(f32)
        b = d[D_LAT + HALF :].astype(f32)
        base += D_NOPE
        ft[base : base + HALF, :] = (a * cos + b * sin).astype(bf16)
        ft[base + HALF : base + D_ROPE, :] = (b * cos - a * sin).astype(bf16)
    cg[...] = dot(uq[...], ft[...]).astype(bf16)
    y, xh = place[3], place[4]
    for d in range(N_Y):
        yd = lax.rem(y + d, N_Y)
        for k, h in enumerate((xh, 1 - xh)):
            rows = pl.ds(pl.multiple_of((yd * N_XH + h) * C_COLS, 64), C_COLS)
            for t in range(2):
                outs[d][t, k] = cg[rows, t * TOK : (t + 1) * TOK]


def project(order, place, dss, kts, uk, uq):
    k = np.arange(HALF, dtype=np.float32)[:, None]
    frequency = np.float32(10000.0) ** (-(2.0 * k) / D_ROPE)
    frequency = jnp.asarray(np.broadcast_to(frequency, (HALF, TOK)), f32)
    q_rank = uq.shape[0]
    return pl.pallas_call(
        project_kernel,
        out_shape=(like(2, N_XH, C_COLS, TOK),) * N_Y,
        in_specs=[smem()] * 2 + [vmem()] * (3 + len(dss) + len(kts)),
        out_specs=(vmem(),) * 4,
        scratch_shapes=[pltpu.VMEM((F_ROWS, 2 * TOK), bf16), pltpu.VMEM((q_rank, 2 * TOK), bf16)],
        compiler_params=params(12),
        cost_estimate=cost(4 * HROWS * KEYS * ROW),
        name="project",
    )(order, place, uk, uq, frequency, *held(*dss, *kts))


def gather_kernel(p0, p1, p2, p3, *outs):
    for t in range(2):
        for k in range(N_XH):
            a, c, b, d = (p[t, k].astype(f32) for p in (p0, p1, p2, p3))
            outs[2 * t + k][...] = ((a + c) + (b + d)).astype(bf16)


def gather(*parts):
    return pl.pallas_call(
        gather_kernel,
        out_shape=(like(C_COLS, TOK),) * 4,
        in_specs=[vmem()] * N_Y,
        out_specs=(vmem(),) * 4,
        compiler_params=params(4),
        cost_estimate=cost(0),
        name="gather",
    )(*parts)


def add(*parts):
    return sum(p.astype(f32) for p in parts).astype(bf16)


def per_device(queries, latent_rows, output_grad, up_query, up_key, up_value, block_order):
    coords = [lax.axis_index(a) for a in ("z", "xl", "core", "y", "xh")]
    place = jnp.stack(coords).astype(jnp.int32)

    own = latent_rows.T
    q_other = shift(queries, dcore=1)
    do_other = shift(output_grad, dcore=1)
    kts = [shift(own, dz=dz) if dz else own for dz, _ in SLOTS[:N_Z]]
    qt, gt, done = prologue(queries, q_other, output_grad, do_other, up_value)
    for (dz, _), kt, dx in zip(SLOTS, kts[:], (1, 3, 1, 3)):
        kt = lax.optimization_barrier((kt, done))[0] if dz else kt
        kts.append(shift(kt, dx=dx))

    parts, kt_parts, mine = [], [], ()
    for slots in GROUPS:
        took = kts[slots[0] : slots[-1] + 1]
        e, dp, kt, m, mine = scores(slots, block_order, place, qt, gt, took, mine)
        parts.append((e, dp, m))
        kt_parts.append(kt)
        mine = (mine,)
    mine = mine[0]
    theirs = shift(mine, dcore=1)
    near, far0, far1 = parts
    (dk1, dk3), dss = grads([(*near, 0), (*far0, 0)], mine, theirs, qt, gt)
    (dk0, dk2), more = grads([(*near, 2), (*far1, 0)], mine, theirs, qt, gt)
    dss = *dss, *more

    from_z = [shift(dk, dz=-dz) for dz, dk in ((1, dk1), (3, dk3), (2, dk2))]
    a, b = (add(*(p[i] for p in (dk0, *from_z))) for i in range(N_XL))

    cg = project(block_order, place, dss, kt_parts, up_key, up_query)

    b1, b3, a2 = shift(b, dx=1), shift(b, dx=3), shift(a, dx=2)
    total = ((a.astype(f32) + a2.astype(f32)) + (b1.astype(f32) + b3.astype(f32))).astype(bf16)
    s1, s3, s2 = (shift(total, dy=d).astype(f32) for d in (1, 3, 2))
    total = ((total.astype(f32) + s2) + (s1 + s3)).astype(bf16)

    keep, send, give_keep, give_send = gather(cg[0], *(shift(cg[d], dy=d) for d in (2, 1, 3)))
    got = shift(send, dx=2), shift(give_keep, dcore=1), shift(give_send, dx=2, dcore=1)
    return add(keep, *got).T, total.T


def solution(mesh):
    fine = Mesh(mesh.devices.reshape(N_Y, N_XH, N_Z, N_XL, 2), AXES)
    head, ctx = ("y", "xh"), ("z", "xl", "core")
    in_specs = (
        P(ctx, head),
        P(ctx, None),
        P(ctx, head),
        P(None, head),
        P(head, None, None),
        P(head, None, None),
        P(),
    )
    out_specs = (P(ctx, head), P(ctx, None))
    return jax.shard_map(
        per_device, mesh=fine, in_specs=in_specs, out_specs=out_specs, check_vma=False
    )
```
